32 devices in a mesh: energy: 8 (over y, x, core), atom: 4 (over z).
Axes of the slice: x: 2, y: 2, z: 4, core: 2. Of those that a mesh axis runs over, the one named last changes fastest.
Arguments:
- green_ret: bfloat16 [2, 12, 12, 384, 128], P(None, None, None, ('energy', 'atom')), may hold values from -1.59375 to 1.59375
- broadening: bfloat16 [2, 2, 12, 12, 384, 128], P(None, None, None, None, ('energy', 'atom')), may hold values from -6 to 6
- coupling: float32 [64], replicated, may hold values from 0.01 to 0.1
- occupation: float32 [64], replicated, may hold values from 0.05 to 3
- shifts: int32 [64], replicated, may hold values from 1 to 2, as said below
- neighbours: int32 [128, 34], P('atom'), may hold values from -24 to 151, as said below
- bond_count: int32 [128], P('atom'), may hold values from 17 to 34
- bond_weight: bfloat16 [128, 34], P('atom'), may hold values from -1 to 1
Outputs:
- self_energy: bfloat16 [2, 2, 12, 12, 384, 128], P(None, None, None, None, ('energy', 'atom'))
- polarization: float32 [64, 128], P('energy', 'atom')
The draws below stay inside these ranges and needn't reach their ends.
Inputs may be any that keep to these rules, and one draw needn't show every extreme that they name: `shifts`: each mode's energy in energy steps. `neighbours`: the entries of row a are distinct and lie within 24 of a; entries outside 0 .. 127 name no atom. `bond_count`: the live slots of an atom are the leading ones of its row.
All inputs are finite; a program needn't handle non-finite values.
Results may differ from the reference program's by a relative error of at most 0.0076.
Values may be sent and summed in bfloat16 or wider, within the bound.
A program may use at most 128 MiB of HBM per device.

```python
import math
import jax
import jax.numpy as jnp
from jax import lax

ORB = 12
NEIGH = 34
REACH = 24
MODES = 64
SHIFT = 2
NE = 384
NA = 128


def draw_shifts(key, part):
    values = jax.random.randint(key, (MODES,), 1, SHIFT + 1)
    top_slot = jax.random.randint(jax.random.fold_in(key, 11), (), 0, MODES)
    values = values.at[top_slot].set(SHIFT)
    values = values.at[(top_slot + 1) % MODES].set(1)
    return values.astype(jnp.int32)


def draw_neighbours(key, part):
    width_all = 2 * REACH + 1
    scores = jax.random.randint(key, (NA, width_all), 0, 1 << 20) * width_all
    scores = scores + jnp.arange(width_all, dtype=jnp.int32)[None, :]
    scores = scores.at[0, 0].set(-1)
    scores = scores.at[NA - 1, width_all - 1].set(-1)
    middle = jax.random.randint(jax.random.fold_in(key, 7), (), 0, NA)
    scores = scores.at[middle, width_all - 1].set(-1)
    order = jnp.argsort(scores, axis=1, stable=True).astype(jnp.int32)
    offsets = order[:, :NEIGH] - REACH
    return (jnp.arange(NA, dtype=jnp.int32)[:, None] + offsets).astype(jnp.int32)


def touch_ends(drawn, own_key, low, high):
    spot = [jax.random.randint(jax.random.fold_in(own_key, axis), (), 0, length) for axis, length in enumerate(drawn.shape)]
    main_axis = drawn.shape.index(max(drawn.shape))
    neighbour = spot[:main_axis] + [(spot[main_axis] + 1) % drawn.shape[main_axis]] + spot[main_axis + 1:]
    return drawn.at[tuple(spot)].set(low).at[tuple(neighbour)].set(high)


def level_of(rng, dims, shards, smallest, largest):
    factor_of, own = 1.0, jax.random.fold_in(rng, 6)
    for position, blocks in shards:
        heights = jnp.exp(jax.random.uniform(jax.random.fold_in(own, position), (blocks,), jnp.float32, smallest / len(shards), largest / len(shards)))
        factor_of = factor_of * jnp.repeat(heights, dims[position] // blocks).reshape([-1 if axis == position else 1 for axis in range(len(dims))])
    return factor_of


def normal_values(stream_key, shape, width, limit, split=(), kind=jnp.bfloat16):
    drawn = width * jax.random.normal(stream_key, shape, jnp.float32)
    if split:
        drawn = drawn * level_of(stream_key, shape, split, -0.22, 0.18)
    return jnp.clip(drawn, -limit, limit).astype(kind)


def setup_inputs(seed: int = 0) -> dict:
    key_of = jax.random.split(jax.random.key(seed), 9)
    return {
        "green_ret": normal_values(key_of[0], (2, ORB, ORB, NE, NA), 0.2, 1.59375, ((3, 32),)),
        "broadening": normal_values(key_of[1], (2, 2, ORB, ORB, NE, NA), 1.0, 6.0, ((4, 32),)),
        "coupling": jnp.clip(jnp.exp(jax.random.uniform(key_of[2], (MODES,), jnp.float32, math.log(0.01), math.log(0.1))), 0.01, 0.1),
        "occupation": jnp.clip(jnp.exp(jax.random.uniform(key_of[3], (MODES,), jnp.float32, math.log(0.05), math.log(3.0))), 0.05, 3.0),
        "shifts": draw_shifts(jax.random.fold_in(key_of[8], 71), 0),
        "neighbours": draw_neighbours(jax.random.fold_in(key_of[8], 71), 0),
        "bond_count": touch_ends(jax.random.randint(key_of[6], (NA,), NEIGH // 2, NEIGH + 1), jax.random.fold_in(key_of[6], 1), NEIGH // 2, NEIGH).astype(jnp.int32),
        "bond_weight": normal_values(key_of[7], (NA, NEIGH), NEIGH ** -0.5, 1.0, ((0, 4),)),
    }


PRECISE = lax.Precision.HIGHEST

def complex_times(first, second):

    def product(one, two):
        return jnp.einsum('ikea,kjea->ijea', one, two, precision=PRECISE, preferred_element_type=jnp.float32)
    real_part = product(first[0], second[0]) - product(first[1], second[1])
    imag_part = product(first[0], second[1]) + product(first[1], second[0])
    return jnp.stack([real_part, imag_part])

def times_adjoint(first, second):

    def product(one, two):
        return jnp.einsum('ikea,jkea->ijea', one, two, precision=PRECISE, preferred_element_type=jnp.float32)
    real_part = product(first[0], second[0]) + product(first[1], second[1])
    imag_part = product(first[1], second[0]) - product(first[0], second[1])
    return jnp.stack([real_part, imag_part])

def reference(green_ret, broadening, coupling, occupation, shifts, neighbours, bond_count, bond_weight):
    retarded = green_ret.astype(jnp.float32)
    results = []
    for species in range(2):
        halfway = complex_times(retarded, broadening[species].astype(jnp.float32))
        results.append(times_adjoint(halfway, retarded))
    keldysh = jnp.stack(results).astype(jnp.bfloat16)
    levels = jnp.arange(1, SHIFT + 1, dtype=jnp.int32)
    onehot = (shifts[:, None] == levels[None, :]).astype(jnp.float32)
    emission16 = jnp.dot(coupling * (occupation + 1.0), onehot, precision=PRECISE).astype(jnp.bfloat16)
    absorption16 = jnp.dot(coupling * occupation, onehot, precision=PRECISE).astype(jnp.bfloat16)
    emission = lax.optimization_barrier(emission16).astype(jnp.float32)
    absorption = lax.optimization_barrier(absorption16).astype(jnp.float32)
    padded = jnp.pad(keldysh.astype(jnp.float32), [(0, 0)] * 4 + [(SHIFT, SHIFT), (0, 0)])
    lesser = jnp.zeros(keldysh.shape[1:], jnp.float32)
    greater = jnp.zeros(keldysh.shape[1:], jnp.float32)
    for offset in range(1, SHIFT + 1):
        higher = padded[:, :, :, :, SHIFT + offset:SHIFT + offset + NE]
        behind = padded[:, :, :, :, SHIFT - offset:SHIFT - offset + NE]
        lesser = lesser + emission[offset - 1] * higher[0] + absorption[offset - 1] * behind[0]
        greater = greater + absorption[offset - 1] * higher[1] + emission[offset - 1] * behind[1]
    shifted = jnp.stack([lesser, greater]).astype(jnp.bfloat16)
    atom_ids = jnp.arange(NA, dtype=jnp.int32)
    active = jnp.arange(NEIGH, dtype=jnp.int32)[None, :] < bond_count[:, None]
    weights = jnp.where(active, bond_weight.astype(jnp.float32), jnp.float32(0.0))
    matches = (neighbours[:, :, None] == atom_ids[None, None, :]).astype(jnp.float32)
    coupling_matrix = jnp.einsum('ak,akb->ab', weights, matches, precision=PRECISE)
    self_energy = jnp.einsum('kcijeb,ab->kcijea', shifted.astype(jnp.float32), coupling_matrix, precision=PRECISE).astype(jnp.bfloat16)
    lower = jnp.pad(keldysh[1].astype(jnp.float32), [(0, 0)] * 3 + [(SHIFT, 0), (0, 0)])
    parity = jnp.array([1.0, -1.0], jnp.float32).reshape(2, 1, 1, 1, 1)
    signed = keldysh[0].astype(jnp.float32) * parity
    totals = []
    for offset in range(1, SHIFT + 1):
        before = lower[:, :, :, SHIFT - offset:SHIFT - offset + NE]
        totals.append(jnp.einsum('cijea,cjiea->a', signed, before, precision=PRECISE))
    traces = jnp.stack(totals)
    polarization = coupling[:, None] * jnp.dot(onehot, traces, precision=PRECISE) / math.sqrt(NE)
    return (self_energy, polarization)
```

```python
import functools
import math

import jax
import jax.numpy as jnp
from jax import lax
from jax.experimental import pallas as pl
from jax.experimental.pallas import tpu as pltpu
from jax.sharding import PartitionSpec as P

SHIFT = 2
LANES = 128
ROWS = 8
IBLOCK = 3
JBLOCK = 4
MESH = pl.DeviceIdType.MESH


def ceil_to(value, step):
    return -(-value // step) * step


def pieces(first, count):
    parts, done = [], 0
    while done < count:
        tile, row = divmod(first + done, ROWS)
        size = min(ROWS - row, count - done)
        parts.append((tile, row, size, done))
        done += size
    return parts


def kernel(
    ne, nz, orb, energies, atoms, modes, slots,
    green, broad, coupling, occupation, shifts, count, neighbours, weight,
    out, pol,
    gv, sv, gf, sf, hf, ext, edge, send, recv, bonds, mixing, first, second,
    g_sem, s_sem, send_sem, recv_sem, bsend, brecv, fsend, frecv, ssend, srecv,
):
    e = lax.axis_index("energy")
    z = lax.axis_index("atom")
    chunks = atoms // LANES
    tiles = pl.cdiv(2 * energies, ROWS)
    stride = ceil_to(energies + 2 * SHIFT, ROWS)
    out_rows = ceil_to(energies, ROWS)
    iblocks, jblocks = orb // IBLOCK, orb // JBLOCK
    tile_width = atoms // nz
    last = ne * nz - 1
    place = e * nz + z

    def at_place(index):
        return {"energy": index // nz, "atom": lax.rem(index, nz)}

    above = at_place(lax.rem(place + 1, ne * nz))
    below = at_place(lax.rem(place + last, ne * nz))

    def input_copies(lc):
        lanes = pl.ds(pl.multiple_of(lc * LANES, LANES), LANES)
        return (
            pltpu.make_async_copy(green.at[:, :, :, :, lanes], gv, g_sem),
            pltpu.make_async_copy(broad.at[:, :, :, :, :, lanes], sv, s_sem),
        )

    if chunks == 1:
        for copy in input_copies(0):
            copy.start()

    barrier = pltpu.get_barrier_semaphore()
    pl.semaphore_signal(barrier, inc=1, device_id=above, device_id_type=MESH)
    pl.semaphore_signal(barrier, inc=1, device_id=below, device_id_type=MESH)

    @pl.loop(1, nz)
    def _(step):
        target = {"energy": e, "atom": lax.rem(z + step, nz)}
        pl.semaphore_signal(barrier, inc=1, device_id=target, device_id_type=MESH)

    @pl.loop(1, ne)
    def _(step):
        target = {"energy": lax.rem(e + step, ne), "atom": z}
        pl.semaphore_signal(barrier, inc=1, device_id=target, device_id_type=MESH)

    row_id = lax.broadcasted_iota(jnp.int32, (tile_width, slots), 0)
    slot_id = lax.broadcasted_iota(jnp.int32, (tile_width, slots), 1)
    live = jnp.zeros((tile_width, slots), jnp.int32)
    for row in range(tile_width):
        live = jnp.where(row_id == row, count[row], live)
    live_weight = jnp.where(slot_id < live, weight[...].astype(jnp.float32), 0.0)
    named = neighbours[...]
    atom_id = lax.broadcasted_iota(jnp.int32, (tile_width, atoms), 1)
    bond_rows = jnp.zeros((tile_width, atoms), jnp.float32)
    for slot in range(slots):
        bond_rows += jnp.where(
            named[:, slot : slot + 1] == atom_id, live_weight[:, slot : slot + 1], 0.0
        )
    bonds[z] = bond_rows.astype(jnp.bfloat16)

    def add_mode(q, sums):
        strength, filling, shift = coupling[q], occupation[q], shifts[q]
        emit, absorb = strength * (filling + 1.0), strength * filling
        return tuple(
            total + jnp.where(shift == level, term, 0.0)
            for level, (pair) in enumerate(zip(sums[::2], sums[1::2]), 1)
            for total, term in zip(pair, (emit, absorb))
        )

    sums = lax.fori_loop(0, modes, add_mode, (jnp.float32(0.0),) * (2 * SHIFT))
    rounded = [
        jnp.full((out_rows, LANES), total, jnp.float32).astype(jnp.bfloat16).astype(jnp.float32)
        for total in sums
    ]
    emission, absorption = rounded[::2], rounded[1::2]

    pl.semaphore_wait(barrier, 2 + (nz - 1) + (ne - 1))

    def bond_copy(step):
        return pltpu.make_async_remote_copy(
            src_ref=bonds.at[z],
            dst_ref=bonds.at[z],
            send_sem=bsend.at[step],
            recv_sem=brecv.at[step],
            device_id={"energy": e, "atom": lax.rem(z + step, nz)},
            device_id_type=MESH,
        )

    @pl.loop(1, nz)
    def _(step):
        bond_copy(step).start()

    def halo_copy(lc, ib, side):
        return pltpu.make_async_remote_copy(
            src_ref=send.at[lc, side, ib],
            dst_ref=recv.at[lc, side, ib],
            send_sem=send_sem.at[lc, side, ib],
            recv_sem=recv_sem.at[lc, side, ib],
            device_id=above if side else below,
            device_id_type=MESH,
        )

    def store_forms(target, index, forms):
        for form, value in enumerate(forms):
            for tile in range(tiles):
                low, high = tile * ROWS, min((tile + 1) * ROWS, 2 * energies)
                target[tile, form, index, :, 0 : high - low] = value[:, low:high]

    def keldysh_chunk(lc):
        g_copy, s_copy = input_copies(lc)
        if chunks > 1:
            g_copy.start()
            s_copy.start()
        g_copy.wait()

        @pl.loop(0, orb)
        def _(i):
            real = gv[0, i].astype(jnp.float32)
            imag = gv[1, i].astype(jnp.float32)
            real = jnp.concatenate([real, real], axis=1)
            imag = jnp.concatenate([imag, imag], axis=1)
            store_forms(gf, i, (real, imag, real + imag, real - imag))

        s_copy.wait()

        @pl.loop(0, orb)
        def _(i):
            real = [sv[k, 0, i].astype(jnp.float32) for k in range(2)]
            imag = [sv[k, 1, i].astype(jnp.float32) for k in range(2)]
            real = jnp.concatenate(real, axis=1)
            imag = jnp.concatenate(imag, axis=1)
            store_forms(sf, i, (real, imag, real + imag))

        @pl.loop(0, iblocks)
        def _(ib):
            irows = pl.ds(ib * IBLOCK, IBLOCK)

            @pl.loop(0, tiles * jblocks)
            def _(step):
                tile, jb = step // jblocks, lax.rem(step, jblocks)
                jrows = pl.ds(jb * JBLOCK, JBLOCK)
                total = [None] * 3
                for inner in range(orb):
                    for form in range(3):
                        term = gf[tile, form, irows, inner][:, None] * sf[tile, form, inner, jrows][None]
                        total[form] = term if inner == 0 else total[form] + term
                real = total[0] - total[1]
                imag = total[2] - total[0] - total[1]
                for form, value in enumerate((real, imag, real + imag)):
                    hf[tile, form, :, jrows] = value

            @pl.loop(0, jblocks)
            def _(jb):
                jrows = pl.ds(jb * JBLOCK, JBLOCK)
                for tile in range(tiles):
                    total = [None] * 3
                    for inner in range(orb):
                        for form, other in enumerate((0, 1, 3)):
                            term = hf[tile, form, :, inner][:, None] * gf[tile, other, jrows, inner][None]
                            total[form] = term if inner == 0 else total[form] + term
                    parts = (total[0] + total[1], total[2] - total[0] + total[1])
                    for c, value in enumerate(parts):
                        for k in range(2):
                            for t, row, size, done in pieces(k * energies, energies):
                                if t == tile:
                                    start = k * stride + SHIFT + done
                                    ext[lc, c, irows, jrows, start : start + size] = value[
                                        :, :, row : row + size
                                    ]
                            for side, begin in enumerate((0, energies - SHIFT)):
                                for t, row, size, done in pieces(k * energies + begin, SHIFT):
                                    if t == tile:
                                        for j in range(JBLOCK):
                                            start = (j * 2 + k) * SHIFT + done
                                            edge[side, c, :, jb, start : start + size] = value[
                                                :, j, row : row + size
                                            ]

            for side in range(2):
                send[lc, side, ib] = edge[side].astype(jnp.bfloat16)
                halo_copy(lc, ib, side).start()

    if chunks == 1:
        keldysh_chunk(0)
    else:
        pl.loop(0, chunks)(keldysh_chunk)

    @pl.loop(1, nz)
    def _(step):
        bond_copy(step).wait()

    for lc in range(chunks):
        block = bonds[:, :, lc * LANES : (lc + 1) * LANES].reshape(atoms, LANES)
        mixing[lc] = block.astype(jnp.float32).T.astype(jnp.bfloat16)

    keep_high = (place != last).astype(jnp.float32)
    keep_low = (place != 0).astype(jnp.float32)

    def halo_rows(lc):
        @pl.loop(0, iblocks)
        def _(ib):
            for side in range(2):
                halo_copy(lc, ib, side).wait()

            @pl.loop(0, 2 * IBLOCK)
            def _(step):
                c, i = step // IBLOCK, lax.rem(step, IBLOCK)
                for side, keep in enumerate((keep_high, keep_low)):
                    rows = recv[lc, side, ib, c, i].astype(jnp.float32) * keep
                    for k in range(2):
                        start = k * stride + (0 if side else SHIFT + energies)
                        for j in range(orb):
                            row = ((j % JBLOCK) * 2 + k) * SHIFT
                            ext[lc, c, ib * IBLOCK + i, j, start : start + SHIFT] = rows[
                                j // JBLOCK, row : row + SHIFT
                            ]

    if chunks == 1:
        halo_rows(0)
    else:
        pl.loop(0, chunks)(halo_rows)

    def traces(lc):
        def add_row(c, i, totals):
            ahead = ext[lc, c, i, :, SHIFT : SHIFT + energies]
            result = []
            for offset, total in enumerate(totals, 1):
                start = stride + SHIFT - offset
                term = jnp.sum(ahead * ext[lc, c, :, i, start : start + energies], axis=0)
                result.append(total - term if c else total + term)
            return tuple(result)

        totals = (jnp.zeros((energies, LANES), jnp.float32),) * SHIFT
        for c in range(2):
            totals = lax.fori_loop(0, orb, functools.partial(add_row, c), totals)
        first[0, lc] = jnp.zeros((ROWS, LANES), jnp.float32)
        for offset, total in enumerate(totals):
            first[0, lc, offset : offset + 1] = jnp.sum(total, axis=0, keepdims=True)

    if chunks == 1:
        traces(0)
    else:
        pl.loop(0, chunks)(traces)

    def first_copy(step):
        return pltpu.make_async_remote_copy(
            src_ref=first.at[0],
            dst_ref=first.at[step],
            send_sem=fsend.at[step],
            recv_sem=frecv.at[step],
            device_id={"energy": e, "atom": lax.rem(z + step, nz)},
            device_id_type=MESH,
        )

    def second_copy(step):
        return pltpu.make_async_remote_copy(
            src_ref=second.at[0],
            dst_ref=second.at[step],
            send_sem=ssend.at[step],
            recv_sem=srecv.at[step],
            device_id={"energy": lax.rem(e + step, ne), "atom": z},
            device_id_type=MESH,
        )

    def self_energy(c):
        @pl.loop(0, orb)
        def _(i):
            for k in range(2):
                upward, downward = (emission, absorption) if k == 0 else (absorption, emission)
                mixed = None
                for lc in range(chunks):
                    total = None
                    for offset in range(1, SHIFT + 1):
                        for sign, factor in ((1, upward[offset - 1]), (-1, downward[offset - 1])):
                            start = k * stride + SHIFT + sign * offset
                            term = factor[None] * ext[lc, c, i, :, start : start + out_rows]
                            total = term if total is None else total + term
                    flat = total.reshape(orb * out_rows, LANES).astype(jnp.bfloat16)
                    product = jnp.dot(flat, mixing[lc], preferred_element_type=jnp.float32)
                    mixed = product if mixed is None else mixed + product
                mixed = mixed.reshape(orb, out_rows, atoms)
                out[k, c, i] = mixed[:, :energies].astype(jnp.bfloat16)

    @pl.loop(1, nz)
    def _(step):
        first_copy(step).start()

    self_energy(0)

    @pl.loop(1, nz)
    def _(step):
        first_copy(step).wait()

    second[0] = jnp.sum(first[...], axis=0)

    @pl.loop(1, ne)
    def _(step):
        second_copy(step).start()

    self_energy(1)

    @pl.loop(1, ne)
    def _(step):
        second_copy(step).wait()

    summed = jnp.sum(second[...], axis=0)
    own = jnp.zeros((ROWS, tile_width), jnp.float32)
    for tile in range(nz):
        lc, lane = divmod(tile * tile_width, LANES)
        own = jnp.where(z == tile, summed[lc, :, lane : lane + tile_width], own)
    share = modes // ne
    scale = 1.0 / math.sqrt(energies * ne * nz)
    for row in range(share):
        mode = e * share + row
        shift = shifts[mode]
        line = jnp.zeros((1, tile_width), jnp.float32)
        for level in range(1, SHIFT + 1):
            line += jnp.where(shift == level, 1.0, 0.0) * own[level - 1 : level]
        pol[row : row + 1] = line * (coupling[mode] * scale)


def local(ne, nz, green_ret, broadening, coupling, occupation, shifts, neighbours, bond_count, bond_weight):
    orb, energies, atoms = green_ret.shape[1], green_ret.shape[3], green_ret.shape[4]
    modes, slots = coupling.shape[0], neighbours.shape[1]
    tile_width = neighbours.shape[0]
    chunks = atoms // LANES
    tiles = pl.cdiv(2 * energies, ROWS)
    stride = ceil_to(energies + 2 * SHIFT, ROWS)
    out_rows = ceil_to(energies, ROWS)
    ext_rows = ceil_to(stride + out_rows + 2 * SHIFT, ROWS)
    iblocks, jblocks = orb // IBLOCK, orb // JBLOCK
    edge_shape = (2, IBLOCK, jblocks, JBLOCK * 2 * SHIFT, LANES)
    halo_shape = (chunks, 2, iblocks) + edge_shape
    dma = pltpu.SemaphoreType.DMA
    vmem = pl.BlockSpec(memory_space=pltpu.VMEM)
    smem = pl.BlockSpec(memory_space=pltpu.SMEM)
    anywhere = pl.BlockSpec(memory_space=pl.ANY)
    call = pl.pallas_call(
        functools.partial(kernel, ne, nz, orb, energies, atoms, modes, slots),
        out_shape=(
            jax.ShapeDtypeStruct(broadening.shape, jnp.bfloat16),
            jax.ShapeDtypeStruct((modes // ne, tile_width), jnp.float32),
        ),
        in_specs=[anywhere, anywhere, smem, smem, smem, smem, vmem, vmem],
        out_specs=(vmem, vmem),
        scratch_shapes=[
            pltpu.VMEM((2, orb, orb, energies, LANES), jnp.bfloat16),
            pltpu.VMEM((2, 2, orb, orb, energies, LANES), jnp.bfloat16),
            pltpu.VMEM((tiles, 4, orb, orb, ROWS, LANES), jnp.float32),
            pltpu.VMEM((tiles, 3, orb, orb, ROWS, LANES), jnp.float32),
            pltpu.VMEM((tiles, 3, IBLOCK, orb, ROWS, LANES), jnp.float32),
            pltpu.VMEM((chunks, 2, orb, orb, ext_rows, LANES), jnp.float32),
            pltpu.VMEM((2,) + edge_shape, jnp.float32),
            pltpu.VMEM(halo_shape, jnp.bfloat16),
            pltpu.VMEM(halo_shape, jnp.bfloat16),
            pltpu.VMEM((nz, tile_width, atoms), jnp.bfloat16),
            pltpu.VMEM((chunks, LANES, atoms), jnp.bfloat16),
            pltpu.VMEM((nz, chunks, ROWS, LANES), jnp.float32),
            pltpu.VMEM((ne, chunks, ROWS, LANES), jnp.float32),
            dma,
            dma,
            dma((chunks, 2, iblocks)),
            dma((chunks, 2, iblocks)),
            dma((nz,)),
            dma((nz,)),
            dma((nz,)),
            dma((nz,)),
            dma((ne,)),
            dma((ne,)),
        ],
        compiler_params=pltpu.CompilerParams(
            collective_id=0, has_side_effects=True, vmem_limit_bytes=60 * 1024 * 1024
        ),
    )
    return call(green_ret, broadening, coupling, occupation, shifts, bond_count, neighbours, bond_weight)


def solution(mesh):
    in_specs = (
        P(None, None, None, ("energy", "atom"), None),
        P(None, None, None, None, ("energy", "atom"), None),
        P(),
        P(),
        P(),
        P("atom", None),
        P("atom"),
        P("atom", None),
    )
    out_specs = (P(None, None, None, None, ("energy", "atom"), None), P("energy", "atom"))
    body = functools.partial(local, mesh.shape["energy"], mesh.shape["atom"])
    return jax.shard_map(body, mesh=mesh, in_specs=in_specs, out_specs=out_specs, check_vma=False)
```

```python
import functools
import math

import jax
import jax.numpy as jnp
from jax import lax
from jax.experimental import pallas as pl
from jax.experimental.pallas import tpu as pltpu
from jax.sharding import PartitionSpec as P

SHIFT = 2
LANES = 128
ROWS = 8
IBLOCK = 3
JBLOCK = 4
MESH = pl.DeviceIdType.MESH


def ceil_to(value, step):
    return -(-value // step) * step


def pieces(first, count):
    parts, done = [], 0
    while done < count:
        tile, row = divmod(first + done, ROWS)
        size = min(ROWS - row, count - done)
        parts.append((tile, row, size, done))
        done += size
    return parts


def keldysh_kernel(
    ne, nz, orb, energies, atoms, modes, slots,
    green, broad, coupling, occupation, shifts, count, neighbours, weight,
    shifted, mixing, summed,
    gv, sv, plain, gf, sf, hf, ext, edge, send, recv, bonds, first, second,
    g_sem, s_sem, send_sem, recv_sem, bsend, brecv, fsend, frecv, ssend, srecv,
):
    e = lax.axis_index("energy")
    z = lax.axis_index("atom")
    chunks = atoms // LANES
    pair_rows = 2 * energies
    tiles = pl.cdiv(pair_rows, ROWS)
    halo = 2 * SHIFT
    out_rows = ceil_to(pair_rows, ROWS)
    iblocks, jblocks = orb // IBLOCK, orb // JBLOCK
    tile_width = atoms // nz
    last = ne * nz - 1
    place = e * nz + z

    def at_place(index):
        return {"energy": index // nz, "atom": lax.rem(index, nz)}

    above = at_place(lax.rem(place + 1, ne * nz))
    below = at_place(lax.rem(place + last, ne * nz))

    def input_copies(lc):
        lanes = pl.ds(pl.multiple_of(lc * LANES, LANES), LANES)
        return (
            pltpu.make_async_copy(green.at[:, :, :, lanes], gv, g_sem),
            pltpu.make_async_copy(broad.at[:, :, :, :, lanes], sv, s_sem),
        )

    if chunks == 1:
        for copy in input_copies(0):
            copy.start()

    barrier = pltpu.get_barrier_semaphore()
    pl.semaphore_signal(barrier, inc=1, device_id=above, device_id_type=MESH)
    pl.semaphore_signal(barrier, inc=1, device_id=below, device_id_type=MESH)

    @pl.loop(1, nz)
    def _(step):
        target = {"energy": e, "atom": lax.rem(z + step, nz)}
        pl.semaphore_signal(barrier, inc=1, device_id=target, device_id_type=MESH)

    @pl.loop(1, ne)
    def _(step):
        target = {"energy": lax.rem(e + step, ne), "atom": z}
        pl.semaphore_signal(barrier, inc=1, device_id=target, device_id_type=MESH)

    row_id = lax.broadcasted_iota(jnp.int32, (tile_width, slots), 0)
    slot_id = lax.broadcasted_iota(jnp.int32, (tile_width, slots), 1)
    live = jnp.zeros((tile_width, slots), jnp.int32)
    for row in range(tile_width):
        live = jnp.where(row_id == row, count[row], live)
    live_weight = jnp.where(slot_id < live, weight[...].astype(jnp.float32), 0.0)
    named = neighbours[...]
    atom_id = lax.broadcasted_iota(jnp.int32, (tile_width, atoms), 1)
    bond_rows = jnp.zeros((tile_width, atoms), jnp.float32)
    for slot in range(slots):
        bond_rows += jnp.where(
            named[:, slot : slot + 1] == atom_id, live_weight[:, slot : slot + 1], 0.0
        )
    bonds[z] = bond_rows.astype(jnp.bfloat16)

    def add_mode(q, sums):
        strength, filling, shift = coupling[q], occupation[q], shifts[q]
        emit, absorb = strength * (filling + 1.0), strength * filling
        return tuple(
            total + jnp.where(shift == level, term, 0.0)
            for level, pair in enumerate(zip(sums[::2], sums[1::2]), 1)
            for total, term in zip(pair, (emit, absorb))
        )

    sums = lax.fori_loop(0, modes, add_mode, (jnp.float32(0.0),) * (2 * SHIFT))
    rounded = [
        jnp.full((out_rows, LANES), total, jnp.float32).astype(jnp.bfloat16).astype(jnp.float32)
        for total in sums
    ]
    emission, absorption = rounded[::2], rounded[1::2]

    def bond_copy(step):
        return pltpu.make_async_remote_copy(
            src_ref=bonds.at[z],
            dst_ref=bonds.at[z],
            send_sem=bsend.at[step],
            recv_sem=brecv.at[step],
            device_id={"energy": e, "atom": lax.rem(z + step, nz)},
            device_id_type=MESH,
        )

    def halo_copy(lc, ib, side):
        return pltpu.make_async_remote_copy(
            src_ref=send.at[lc, side, ib],
            dst_ref=recv.at[lc, side, ib],
            send_sem=send_sem.at[lc, side, ib],
            recv_sem=recv_sem.at[lc, side, ib],
            device_id=above if side else below,
            device_id_type=MESH,
        )

    def store_forms(target, index, count_of):
        for tile in range(tiles):
            low = tile * ROWS
            size = min(ROWS, pair_rows - low)
            real = plain[:, pl.ds(2 * low, size, stride=2)]
            imag = plain[:, pl.ds(2 * low + 1, size, stride=2)]
            forms = (real, imag, real + imag, real - imag)
            for form in range(count_of):
                target[tile, form, index, :, 0:size] = forms[form]

    def prepare(lc):
        g_copy, s_copy = input_copies(lc)
        if chunks > 1:
            g_copy.start()
            s_copy.start()
        g_copy.wait()

        @pl.loop(0, orb)
        def _(i):
            block = gv[i].astype(jnp.float32)
            plain[:, 0:pair_rows] = block
            plain[:, pair_rows : 2 * pair_rows] = block
            store_forms(gf, i, 4)

        s_copy.wait()

        @pl.loop(0, orb)
        def _(i):
            for k in range(2):
                plain[:, k * pair_rows : (k + 1) * pair_rows] = sv[k, i].astype(jnp.float32)
            store_forms(sf, i, 3)

    def keldysh_chunk(lc):
        if chunks > 1:
            prepare(lc)

        @pl.loop(0, iblocks)
        def _(ib):
            irows = pl.ds(ib * IBLOCK, IBLOCK)

            @pl.loop(0, tiles * jblocks)
            def _(step):
                tile, jb = step // jblocks, lax.rem(step, jblocks)
                jrows = pl.ds(jb * JBLOCK, JBLOCK)
                total = [None] * 3
                for inner in range(orb):
                    for form in range(3):
                        term = gf[tile, form, irows, inner][:, None] * sf[tile, form, inner, jrows][None]
                        total[form] = term if inner == 0 else total[form] + term
                real = total[0] - total[1]
                imag = total[2] - total[0] - total[1]
                for form, value in enumerate((real, imag, real + imag)):
                    hf[tile, form, :, jrows] = value

            @pl.loop(0, jblocks)
            def _(jb):
                jrows = pl.ds(jb * JBLOCK, JBLOCK)
                for tile in range(tiles):
                    total = [None] * 3
                    for inner in range(orb):
                        for form, other in enumerate((0, 1, 3)):
                            term = hf[tile, form, :, inner][:, None] * gf[tile, other, jrows, inner][None]
                            total[form] = term if inner == 0 else total[form] + term
                    parts = (total[0] + total[1], total[2] - total[0] + total[1])
                    for c, value in enumerate(parts):
                        for k in range(2):
                            for t, row, size, done in pieces(k * energies, energies):
                                if t == tile:
                                    start = halo + 2 * done + c
                                    ext[lc, k, irows, jrows, pl.ds(start, size, stride=2)] = value[
                                        :, :, row : row + size
                                    ]

            for side, start in enumerate((halo, pair_rows)):
                for k in range(2):
                    for j in range(orb):
                        row = (j % JBLOCK) * halo
                        edge[side, k, :, j // JBLOCK, row : row + halo] = ext[
                            lc, k, irows, j, start : start + halo
                        ]
                send[lc, side, ib] = edge[side].astype(jnp.bfloat16)
                halo_copy(lc, ib, side).start()

    if chunks == 1:
        prepare(0)
    pl.semaphore_wait(barrier, 2 + (nz - 1) + (ne - 1))

    @pl.loop(1, nz)
    def _(step):
        bond_copy(step).start()

    if chunks == 1:
        keldysh_chunk(0)
    else:
        pl.loop(0, chunks)(keldysh_chunk)

    def inner_traces(lc):
        def add_row(i, totals):
            result = []
            for offset, total in enumerate(totals, 1):
                size = pair_rows - 2 * offset
                ahead = ext[lc, 0, i, :, halo + 2 * offset : halo + pair_rows]
                behind = ext[lc, 1, :, i, halo : halo + size]
                result.append(total + jnp.sum(ahead * behind, axis=0))
            return tuple(result)

        starts = tuple(
            jnp.zeros((pair_rows - 2 * offset, LANES), jnp.float32)
            for offset in range(1, SHIFT + 1)
        )
        return lax.fori_loop(0, orb, add_row, starts)

    def signed_sum(total):
        parity = lax.rem(lax.broadcasted_iota(jnp.int32, total.shape, 0), 2)
        return jnp.sum(jnp.where(parity == 0, total, -total), axis=0, keepdims=True)

    def store_inner(lc):
        first[0, lc] = jnp.zeros((ROWS, LANES), jnp.float32)
        for offset, total in enumerate(inner_traces(lc)):
            if total.shape[0]:
                first[0, lc, offset : offset + 1] = signed_sum(total)

    if chunks == 1:
        store_inner(0)
    else:
        pl.loop(0, chunks)(store_inner)

    @pl.loop(1, nz)
    def _(step):
        bond_copy(step).wait()

    for lc in range(chunks):
        block = bonds[:, :, lc * LANES : (lc + 1) * LANES].reshape(atoms, LANES)
        mixing[lc] = block.astype(jnp.float32).T.astype(jnp.bfloat16)

    keep_high = (place != last).astype(jnp.float32)
    keep_low = (place != 0).astype(jnp.float32)

    def halo_rows(lc):
        def take_block(ib, totals):
            for side in range(2):
                halo_copy(lc, ib, side).wait()
            irows = pl.ds(ib * IBLOCK, IBLOCK)
            for side, keep in enumerate((keep_high, keep_low)):
                start = 0 if side else halo + pair_rows
                for k in range(2):
                    rows = recv[lc, side, ib, k].astype(jnp.float32) * keep
                    for j in range(orb):
                        row = (j % JBLOCK) * halo
                        ext[lc, k, irows, j, start : start + halo] = rows[
                            :, j // JBLOCK, row : row + halo
                        ]
            totals = list(totals)
            for step in range(IBLOCK):
                i = ib * IBLOCK + step
                for offset in range(1, SHIFT + 1):
                    ahead = ext[lc, 0, :, i, halo : halo + 2 * offset]
                    behind = ext[lc, 1, i, :, halo - 2 * offset : halo]
                    totals[offset - 1] += jnp.sum(ahead * behind, axis=0)
            return tuple(totals)

        starts = tuple(
            jnp.zeros((2 * offset, LANES), jnp.float32) for offset in range(1, SHIFT + 1)
        )
        totals = lax.fori_loop(0, iblocks, take_block, starts)
        for offset, total in enumerate(totals):
            first[0, lc, offset : offset + 1] += signed_sum(total)

    if chunks == 1:
        halo_rows(0)
    else:
        pl.loop(0, chunks)(halo_rows)

    def first_copy(step):
        return pltpu.make_async_remote_copy(
            src_ref=first.at[0],
            dst_ref=first.at[step],
            send_sem=fsend.at[step],
            recv_sem=frecv.at[step],
            device_id={"energy": e, "atom": lax.rem(z + step, nz)},
            device_id_type=MESH,
        )

    def second_copy(step):
        return pltpu.make_async_remote_copy(
            src_ref=second.at[0],
            dst_ref=second.at[step],
            send_sem=ssend.at[step],
            recv_sem=srecv.at[step],
            device_id={"energy": lax.rem(e + step, ne), "atom": z},
            device_id_type=MESH,
        )

    def shift_energies(k):
        upward, downward = (emission, absorption) if k == 0 else (absorption, emission)

        @pl.loop(0, chunks * orb)
        def _(step):
            lc, i = step // orb, lax.rem(step, orb)
            total = None
            for offset in range(1, SHIFT + 1):
                for sign, factor in ((1, upward[offset - 1]), (-1, downward[offset - 1])):
                    start = halo + 2 * sign * offset
                    term = factor[None] * ext[lc, k, i, :, start : start + out_rows]
                    total = term if total is None else total + term
            flat = total.reshape(orb * out_rows, LANES)
            shifted[k, lc, i] = flat.astype(jnp.bfloat16)

    @pl.loop(1, nz)
    def _(step):
        first_copy(step).start()

    shift_energies(0)

    @pl.loop(1, nz)
    def _(step):
        first_copy(step).wait()

    second[0] = jnp.sum(first[...], axis=0)

    @pl.loop(1, ne)
    def _(step):
        second_copy(step).start()

    shift_energies(1)

    @pl.loop(1, ne)
    def _(step):
        second_copy(step).wait()

    summed[...] = jnp.sum(second[...], axis=0)


def mixing_kernel(ne, nz, orb, energies, atoms, modes, coupling, shifts, shifted, mixing, summed, out, pol):
    chunks = atoms // LANES
    pair_rows = 2 * energies
    out_rows = ceil_to(pair_rows, ROWS)
    for row in range(IBLOCK):
        mixed = None
        for lc in range(chunks):
            product = jnp.dot(
                shifted[0, lc, row], mixing[lc], preferred_element_type=jnp.float32
            )
            mixed = product if mixed is None else mixed + product
        mixed = mixed.reshape(orb, out_rows, atoms)
        out[0, row] = mixed[:, :pair_rows].astype(jnp.bfloat16)

    @pl.when((pl.program_id(0) == 0) & (pl.program_id(1) == 0))
    def _():
        e = lax.axis_index("energy")
        z = lax.axis_index("atom")
        tile_width = atoms // nz
        own = jnp.zeros((ROWS, tile_width), jnp.float32)
        for tile in range(nz):
            lc, lane = divmod(tile * tile_width, LANES)
            own = jnp.where(z == tile, summed[lc, :, lane : lane + tile_width], own)
        share = modes // ne
        scale = 1.0 / math.sqrt(energies * ne * nz)
        for row in range(share):
            mode = e * share + row
            shift = shifts[mode]
            line = jnp.zeros((1, tile_width), jnp.float32)
            for level in range(1, SHIFT + 1):
                line += jnp.where(shift == level, 1.0, 0.0) * own[level - 1 : level]
            pol[row : row + 1] = line * (coupling[mode] * scale)


def local(ne, nz, green_ret, broadening, coupling, occupation, shifts, neighbours, bond_count, bond_weight):
    orb, energies, atoms = green_ret.shape[1], green_ret.shape[3], green_ret.shape[4]
    modes, slots = coupling.shape[0], neighbours.shape[1]
    tile_width = neighbours.shape[0]
    chunks = atoms // LANES
    pair_rows = 2 * energies
    tiles = pl.cdiv(pair_rows, ROWS)
    out_rows = ceil_to(pair_rows, ROWS)
    ext_rows = ceil_to(max(pair_rows, out_rows) + 4 * SHIFT, ROWS)
    iblocks, jblocks = orb // IBLOCK, orb // JBLOCK
    edge_shape = (2, IBLOCK, jblocks, JBLOCK * 2 * SHIFT, LANES)
    halo_shape = (chunks, 2, iblocks) + edge_shape
    dma = pltpu.SemaphoreType.DMA
    vmem = pl.BlockSpec(memory_space=pltpu.VMEM)
    smem = pl.BlockSpec(memory_space=pltpu.SMEM)
    anywhere = pl.BlockSpec(memory_space=pl.ANY)
    green = green_ret.transpose(1, 2, 3, 0, 4).reshape(orb, orb, pair_rows, atoms)
    broad = broadening.transpose(0, 2, 3, 4, 1, 5).reshape(2, orb, orb, pair_rows, atoms)
    shifted, mixing, summed = pl.pallas_call(
        functools.partial(keldysh_kernel, ne, nz, orb, energies, atoms, modes, slots),
        out_shape=(
            jax.ShapeDtypeStruct((2, chunks, orb, orb * out_rows, LANES), jnp.bfloat16),
            jax.ShapeDtypeStruct((chunks, LANES, atoms), jnp.bfloat16),
            jax.ShapeDtypeStruct((chunks, ROWS, LANES), jnp.float32),
        ),
        in_specs=[anywhere, anywhere, smem, smem, smem, smem, vmem, vmem],
        out_specs=(vmem, vmem, vmem),
        scratch_shapes=[
            pltpu.VMEM((orb, orb, pair_rows, LANES), jnp.bfloat16),
            pltpu.VMEM((2, orb, orb, pair_rows, LANES), jnp.bfloat16),
            pltpu.VMEM((orb, 2 * pair_rows, LANES), jnp.float32),
            pltpu.VMEM((tiles, 4, orb, orb, ROWS, LANES), jnp.float32),
            pltpu.VMEM((tiles, 3, orb, orb, ROWS, LANES), jnp.float32),
            pltpu.VMEM((tiles, 3, IBLOCK, orb, ROWS, LANES), jnp.float32),
            pltpu.VMEM((chunks, 2, orb, orb, ext_rows, LANES), jnp.float32),
            pltpu.VMEM((2,) + edge_shape, jnp.float32),
            pltpu.VMEM(halo_shape, jnp.bfloat16),
            pltpu.VMEM(halo_shape, jnp.bfloat16),
            pltpu.VMEM((nz, tile_width, atoms), jnp.bfloat16),
            pltpu.VMEM((nz, chunks, ROWS, LANES), jnp.float32),
            pltpu.VMEM((ne, chunks, ROWS, LANES), jnp.float32),
            dma,
            dma,
            dma((chunks, 2, iblocks)),
            dma((chunks, 2, iblocks)),
            dma((nz,)),
            dma((nz,)),
            dma((nz,)),
            dma((nz,)),
            dma((ne,)),
            dma((ne,)),
        ],
        compiler_params=pltpu.CompilerParams(
            collective_id=0, has_side_effects=True, vmem_limit_bytes=48 * 1024 * 1024
        ),
    )(green, broad, coupling, occupation, shifts, bond_count, neighbours, bond_weight)
    out, pol = pl.pallas_call(
        functools.partial(mixing_kernel, ne, nz, orb, energies, atoms, modes),
        grid=(2, iblocks),
        out_shape=(
            jax.ShapeDtypeStruct((2, orb, orb, pair_rows, atoms), jnp.bfloat16),
            jax.ShapeDtypeStruct((modes // ne, tile_width), jnp.float32),
        ),
        in_specs=[
            smem,
            smem,
            pl.BlockSpec((1, chunks, IBLOCK, orb * out_rows, LANES), lambda k, ib: (k, 0, ib, 0, 0)),
            pl.BlockSpec((chunks, LANES, atoms), lambda k, ib: (0, 0, 0)),
            pl.BlockSpec((chunks, ROWS, LANES), lambda k, ib: (0, 0, 0)),
        ],
        out_specs=(
            pl.BlockSpec((1, IBLOCK, orb, pair_rows, atoms), lambda k, ib: (k, ib, 0, 0, 0)),
            pl.BlockSpec((modes // ne, tile_width), lambda k, ib: (0, 0)),
        ),
        compiler_params=pltpu.CompilerParams(vmem_limit_bytes=24 * 1024 * 1024),
    )(coupling, shifts, shifted, mixing, summed)
    self_energy = out.reshape(2, orb, orb, energies, 2, atoms).transpose(0, 4, 1, 2, 3, 5)
    return self_energy, pol


def solution(mesh):
    in_specs = (
        P(None, None, None, ("energy", "atom"), None),
        P(None, None, None, None, ("energy", "atom"), None),
        P(),
        P(),
        P(),
        P("atom", None),
        P("atom"),
        P("atom", None),
    )
    out_specs = (P(None, None, None, None, ("energy", "atom"), None), P("energy", "atom"))
    body = functools.partial(local, mesh.shape["energy"], mesh.shape["atom"])
    return jax.shard_map(body, mesh=mesh, in_specs=in_specs, out_specs=out_specs, check_vma=False)
```

```python
import functools
import math

import jax
import jax.numpy as jnp
from jax import lax
from jax.experimental import pallas as pl
from jax.experimental.pallas import tpu as pltpu
from jax.sharding import PartitionSpec as P

SHIFT = 2
LANES = 128
ROWS = 8
IBLOCK = 3
JBLOCK = 4
MESH = pl.DeviceIdType.MESH


def ceil_to(value, step):
    return -(-value // step) * step


def row_plan(energies):
    inner = energies - 2 * SHIFT
    if inner <= 0:
        return [(0, 0, energies), (1, 0, energies)], 2 * energies
    ends = [(k, start, SHIFT) for k in range(2) for start in (0, energies - SHIFT)]
    return ends + [(k, SHIFT, inner) for k in range(2)], 4 * SHIFT


def pieces(energies):
    parts, place = [], 0
    for k, start, count in row_plan(energies)[0]:
        done = 0
        while done < count:
            tile, row = divmod(place + done, ROWS)
            size = min(ROWS - row, count - done)
            parts.append((tile, row, size, k, start + done))
            done += size
        place += count
    return parts


def keldysh_kernel(
    ne, nz, orb, energies, atoms, modes, slots,
    green, broad, coupling_in, occupation_in, shifts_in, count_in, neighbours_in, weight_in,
    shifted, mixing, share_out,
    gv, sv, plain, gf, sf, hf, ext, edge, send, recv, bonds, first, second,
    coupling, occupation, shifts, count, neighbours, weight, small_sem,
    g_sem, s_sem, send_sem, recv_sem, bsend, brecv, fsend, frecv, ssend, srecv,
):
    e = lax.axis_index("energy")
    z = lax.axis_index("atom")
    chunks = atoms // LANES
    pair_rows = 2 * energies
    tiles = pl.cdiv(pair_rows, ROWS)
    edge_tiles = pl.cdiv(row_plan(energies)[1], ROWS)
    halo = 2 * SHIFT
    out_rows = ceil_to(pair_rows, ROWS)
    iblocks, jblocks = orb // IBLOCK, orb // JBLOCK
    tile_width = atoms // nz
    last = ne * nz - 1
    place = e * nz + z

    def at_place(index):
        return {"energy": index // nz, "atom": lax.rem(index, nz)}

    above = at_place(lax.rem(place + 1, ne * nz))
    below = at_place(lax.rem(place + last, ne * nz))

    def input_copies(lc):
        lanes = pl.ds(pl.multiple_of(lc * LANES, LANES), LANES)
        return (
            pltpu.make_async_copy(green.at[:, :, lanes], gv, g_sem),
            pltpu.make_async_copy(broad.at[:, :, :, lanes], sv, s_sem),
        )

    small_copies = [
        pltpu.make_async_copy(source, target, small_sem.at[index])
        for index, (source, target) in enumerate(
            (
                (neighbours_in, neighbours),
                (weight_in, weight),
                (count_in, count),
                (coupling_in, coupling),
                (occupation_in, occupation),
                (shifts_in, shifts),
            )
        )
    ]
    for copy in small_copies:
        copy.start()
    if chunks == 1:
        for copy in input_copies(0):
            copy.start()

    barrier = pltpu.get_barrier_semaphore()
    pl.semaphore_signal(barrier, inc=1, device_id=above, device_id_type=MESH)
    pl.semaphore_signal(barrier, inc=1, device_id=below, device_id_type=MESH)

    @pl.loop(1, nz)
    def _(step):
        target = {"energy": e, "atom": lax.rem(z + step, nz)}
        pl.semaphore_signal(barrier, inc=1, device_id=target, device_id_type=MESH)

    @pl.loop(1, ne)
    def _(step):
        target = {"energy": lax.rem(e + step, ne), "atom": z}
        pl.semaphore_signal(barrier, inc=1, device_id=target, device_id_type=MESH)

    for copy in small_copies:
        copy.wait()

    row_id = lax.broadcasted_iota(jnp.int32, (tile_width, slots), 0)
    slot_id = lax.broadcasted_iota(jnp.int32, (tile_width, slots), 1)
    live = jnp.zeros((tile_width, slots), jnp.int32)
    for row in range(tile_width):
        live = jnp.where(row_id == row, count[row], live)
    live_weight = jnp.where(slot_id < live, weight[...].astype(jnp.float32), 0.0)
    named = neighbours[...]
    atom_id = lax.broadcasted_iota(jnp.int32, (tile_width, atoms), 1)
    bond_rows = jnp.zeros((tile_width, atoms), jnp.float32)
    for slot in range(slots):
        bond_rows += jnp.where(
            named[:, slot : slot + 1] == atom_id, live_weight[:, slot : slot + 1], 0.0
        )
    bonds[z] = bond_rows.astype(jnp.bfloat16)

    def add_mode(q, sums):
        strength, filling, shift = coupling[q], occupation[q], shifts[q]
        emit, absorb = strength * (filling + 1.0), strength * filling
        return tuple(
            total + jnp.where(shift == level, term, 0.0)
            for level, pair in enumerate(zip(sums[::2], sums[1::2]), 1)
            for total, term in zip(pair, (emit, absorb))
        )

    sums = lax.fori_loop(0, modes, add_mode, (jnp.float32(0.0),) * (2 * SHIFT))
    rounded = [
        jnp.full((out_rows, LANES), total, jnp.float32).astype(jnp.bfloat16).astype(jnp.float32)
        for total in sums
    ]
    emission, absorption = rounded[::2], rounded[1::2]

    def bond_copy(step):
        return pltpu.make_async_remote_copy(
            src_ref=bonds.at[z],
            dst_ref=bonds.at[z],
            send_sem=bsend.at[step],
            recv_sem=brecv.at[step],
            device_id={"energy": e, "atom": lax.rem(z + step, nz)},
            device_id_type=MESH,
        )

    def halo_copy(lc, ib, side):
        return pltpu.make_async_remote_copy(
            src_ref=send.at[lc, side, ib],
            dst_ref=recv.at[lc, side, ib],
            send_sem=send_sem.at[lc, side, ib],
            recv_sem=recv_sem.at[lc, side, ib],
            device_id=above if side else below,
            device_id_type=MESH,
        )

    def store_forms(target, index, count_of):
        for tile in range(tiles):
            low = tile * ROWS
            size = min(ROWS, pair_rows - low)
            real = plain[:, pl.ds(2 * low, size, stride=2)]
            imag = plain[:, pl.ds(2 * low + 1, size, stride=2)]
            forms = (real, imag, real + imag, real - imag)
            for form in range(count_of):
                target[tile, form, index, :, 0:size] = forms[form]

    def spread(blocks):
        begin = 0
        for k, start, size in row_plan(energies)[0]:
            plain[:, begin : begin + 2 * size] = blocks[k][:, 2 * start : 2 * (start + size)]
            begin += 2 * size

    def prepare(lc):
        g_copy, s_copy = input_copies(lc)
        if chunks > 1:
            g_copy.start()
            s_copy.start()
        g_copy.wait()

        @pl.loop(0, orb)
        def _(i):
            block = gv[i].astype(jnp.float32).reshape(orb, pair_rows, LANES)
            spread((block, block))
            store_forms(gf, i, 4)

        s_copy.wait()

        @pl.loop(0, orb)
        def _(i):
            spread(
                [sv[k, i].astype(jnp.float32).reshape(orb, pair_rows, LANES) for k in range(2)]
            )
            store_forms(sf, i, 3)

    def keldysh_chunk(lc):
        if chunks > 1:
            prepare(lc)

        def products(ib, first_tile, last_tile):
            irows = pl.ds(ib * IBLOCK, IBLOCK)

            @pl.loop(0, (last_tile - first_tile) * jblocks)
            def _(step):
                tile, jb = first_tile + step // jblocks, lax.rem(step, jblocks)
                jrows = pl.ds(jb * JBLOCK, JBLOCK)
                total = [None] * 3
                for inner in range(orb):
                    for form in range(3):
                        term = gf[tile, form, irows, inner][:, None] * sf[tile, form, inner, jrows][None]
                        total[form] = term if inner == 0 else total[form] + term
                real = total[0] - total[1]
                imag = total[2] - total[0] - total[1]
                for form, value in enumerate((real, imag, real + imag)):
                    hf[tile, form, :, jrows] = value

            @pl.loop(0, jblocks)
            def _(jb):
                jrows = pl.ds(jb * JBLOCK, JBLOCK)
                for tile in range(first_tile, last_tile):
                    total = [None] * 3
                    for inner in range(orb):
                        for form, other in enumerate((0, 1, 3)):
                            term = hf[tile, form, :, inner][:, None] * gf[tile, other, jrows, inner][None]
                            total[form] = term if inner == 0 else total[form] + term
                    parts = (total[0] + total[1], total[2] - total[0] + total[1])
                    for c, value in enumerate(parts):
                        for t, row, size, k, energy in pieces(energies):
                            if t == tile:
                                start = halo + 2 * energy + c
                                ext[lc, k, irows, jrows, pl.ds(start, size, stride=2)] = value[
                                    :, :, row : row + size
                                ]

        @pl.loop(0, iblocks)
        def _(ib):
            irows = pl.ds(ib * IBLOCK, IBLOCK)
            products(ib, 0, edge_tiles)
            for side, start in enumerate((halo, pair_rows)):
                for k in range(2):
                    for j in range(orb):
                        row = (j % JBLOCK) * halo
                        edge[side, k, :, j // JBLOCK, row : row + halo] = ext[
                            lc, k, irows, j, start : start + halo
                        ]
                send[lc, side, ib] = edge[side].astype(jnp.bfloat16)
                halo_copy(lc, ib, side).start()

        if edge_tiles < tiles:
            @pl.loop(0, iblocks)
            def _(ib):
                products(ib, edge_tiles, tiles)

    if chunks == 1:
        prepare(0)
    pl.semaphore_wait(barrier, 2 + (nz - 1) + (ne - 1))

    @pl.loop(1, nz)
    def _(step):
        bond_copy(step).start()

    if chunks == 1:
        keldysh_chunk(0)
    else:
        pl.loop(0, chunks)(keldysh_chunk)

    def inner_traces(lc):
        def add_row(i, totals):
            result = []
            for offset, total in enumerate(totals, 1):
                size = pair_rows - 2 * offset
                ahead = ext[lc, 0, i, :, halo + 2 * offset : halo + pair_rows]
                behind = ext[lc, 1, :, i, halo : halo + size]
                result.append(total + jnp.sum(ahead * behind, axis=0))
            return tuple(result)

        starts = tuple(
            jnp.zeros((pair_rows - 2 * offset, LANES), jnp.float32)
            for offset in range(1, SHIFT + 1)
        )
        return lax.fori_loop(0, orb, add_row, starts)

    def signed_sum(total):
        parity = lax.rem(lax.broadcasted_iota(jnp.int32, total.shape, 0), 2)
        return jnp.sum(jnp.where(parity == 0, total, -total), axis=0, keepdims=True)

    def store_inner(lc):
        first[0, lc] = jnp.zeros((ROWS, LANES), jnp.float32)
        for offset, total in enumerate(inner_traces(lc)):
            if total.shape[0]:
                first[0, lc, offset : offset + 1] = signed_sum(total)

    if chunks == 1:
        store_inner(0)
    else:
        pl.loop(0, chunks)(store_inner)

    @pl.loop(1, nz)
    def _(step):
        bond_copy(step).wait()

    for lc in range(chunks):
        block = bonds[:, :, lc * LANES : (lc + 1) * LANES].reshape(atoms, LANES)
        mixing[lc] = block.astype(jnp.float32).T.astype(jnp.bfloat16)

    keep_high = (place != last).astype(jnp.float32)
    keep_low = (place != 0).astype(jnp.float32)

    def halo_rows(lc):
        def take_block(ib, totals):
            for side in range(2):
                halo_copy(lc, ib, side).wait()
            irows = pl.ds(ib * IBLOCK, IBLOCK)
            for side, keep in enumerate((keep_high, keep_low)):
                start = 0 if side else halo + pair_rows
                for k in range(2):
                    rows = recv[lc, side, ib, k].astype(jnp.float32) * keep
                    for j in range(orb):
                        row = (j % JBLOCK) * halo
                        ext[lc, k, irows, j, start : start + halo] = rows[
                            :, j // JBLOCK, row : row + halo
                        ]
            totals = list(totals)
            for step in range(IBLOCK):
                i = ib * IBLOCK + step
                for offset in range(1, SHIFT + 1):
                    ahead = ext[lc, 0, :, i, halo : halo + 2 * offset]
                    behind = ext[lc, 1, i, :, halo - 2 * offset : halo]
                    totals[offset - 1] += jnp.sum(ahead * behind, axis=0)
            return tuple(totals)

        starts = tuple(
            jnp.zeros((2 * offset, LANES), jnp.float32) for offset in range(1, SHIFT + 1)
        )
        totals = lax.fori_loop(0, iblocks, take_block, starts)
        for offset, total in enumerate(totals):
            first[0, lc, offset : offset + 1] += signed_sum(total)

    if chunks == 1:
        halo_rows(0)
    else:
        pl.loop(0, chunks)(halo_rows)

    def first_copy(step):
        return pltpu.make_async_remote_copy(
            src_ref=first.at[0],
            dst_ref=first.at[step],
            send_sem=fsend.at[step],
            recv_sem=frecv.at[step],
            device_id={"energy": e, "atom": lax.rem(z + step, nz)},
            device_id_type=MESH,
        )

    def second_copy(step):
        return pltpu.make_async_remote_copy(
            src_ref=second.at[0],
            dst_ref=second.at[step],
            send_sem=ssend.at[step],
            recv_sem=srecv.at[step],
            device_id={"energy": lax.rem(e + step, ne), "atom": z},
            device_id_type=MESH,
        )

    def shift_energies(k):
        upward, downward = (emission, absorption) if k == 0 else (absorption, emission)

        @pl.loop(0, chunks * orb)
        def _(step):
            lc, i = step // orb, lax.rem(step, orb)
            total = None
            for offset in range(1, SHIFT + 1):
                for sign, factor in ((1, upward[offset - 1]), (-1, downward[offset - 1])):
                    start = halo + 2 * sign * offset
                    term = factor[None] * ext[lc, k, i, :, start : start + out_rows]
                    total = term if total is None else total + term
            flat = total.reshape(orb * out_rows, LANES)
            shifted[k, lc, i] = flat.astype(jnp.bfloat16)

    @pl.loop(1, nz)
    def _(step):
        first_copy(step).start()

    shift_energies(0)

    @pl.loop(1, nz)
    def _(step):
        first_copy(step).wait()

    second[0] = jnp.sum(first[...], axis=0)

    @pl.loop(1, ne)
    def _(step):
        second_copy(step).start()

    shift_energies(1)

    @pl.loop(1, ne)
    def _(step):
        second_copy(step).wait()

    summed = jnp.sum(second[...], axis=0)
    own = jnp.zeros((ROWS, tile_width), jnp.float32)
    for tile in range(nz):
        lc, lane = divmod(tile * tile_width, LANES)
        own = jnp.where(z == tile, summed[lc, :, lane : lane + tile_width], own)
    share = modes // ne
    scale = 1.0 / math.sqrt(energies * ne * nz)
    for row in range(share):
        mode = e * share + row
        shift = shifts[mode]
        line = jnp.zeros((1, tile_width), jnp.float32)
        for level in range(1, SHIFT + 1):
            line += jnp.where(shift == level, 1.0, 0.0) * own[level - 1 : level]
        share_out[row : row + 1] = line * (coupling[mode] * scale)


def mixing_kernel(orb, energies, atoms, shifted, mixing, share, out, pol):
    chunks = atoms // LANES
    pair_rows = 2 * energies
    out_rows = ceil_to(pair_rows, ROWS)
    for row in range(out.shape[1]):
        mixed = None
        for lc in range(chunks):
            product = jnp.dot(
                shifted[0, lc, row], mixing[lc], preferred_element_type=jnp.float32
            )
            mixed = product if mixed is None else mixed + product
        if out_rows != pair_rows:
            mixed = mixed.reshape(orb, out_rows, atoms)[:, :pair_rows]
            mixed = mixed.reshape(orb * pair_rows, atoms)
        out[0, row] = mixed.astype(jnp.bfloat16)

    pol[...] = share[...]


def local(ne, nz, green_ret, broadening, coupling, occupation, shifts, neighbours, bond_count, bond_weight):
    orb, energies, atoms = green_ret.shape[1], green_ret.shape[3], green_ret.shape[4]
    modes, slots = coupling.shape[0], neighbours.shape[1]
    tile_width = neighbours.shape[0]
    chunks = atoms // LANES
    pair_rows = 2 * energies
    tiles = pl.cdiv(pair_rows, ROWS)
    out_rows = ceil_to(pair_rows, ROWS)
    ext_rows = ceil_to(max(pair_rows, out_rows) + 4 * SHIFT, ROWS)
    iblocks, jblocks = orb // IBLOCK, orb // JBLOCK
    edge_shape = (2, IBLOCK, jblocks, JBLOCK * 2 * SHIFT, LANES)
    halo_shape = (chunks, 2, iblocks) + edge_shape
    dma = pltpu.SemaphoreType.DMA
    vmem = pl.BlockSpec(memory_space=pltpu.VMEM)
    hbm = pl.BlockSpec(memory_space=pltpu.HBM)
    green = green_ret.transpose(1, 2, 3, 0, 4).reshape(orb, orb * pair_rows, atoms)
    broad = broadening.transpose(0, 2, 3, 4, 1, 5).reshape(2, orb, orb * pair_rows, atoms)
    shifted, mixing, share = pl.pallas_call(
        functools.partial(keldysh_kernel, ne, nz, orb, energies, atoms, modes, slots),
        out_shape=(
            jax.ShapeDtypeStruct((2, chunks, orb, orb * out_rows, LANES), jnp.bfloat16),
            jax.ShapeDtypeStruct((chunks, LANES, atoms), jnp.bfloat16),
            jax.ShapeDtypeStruct((modes // ne, tile_width), jnp.float32),
        ),
        in_specs=[hbm] * 8,
        out_specs=(vmem, vmem, vmem),
        scratch_shapes=[
            pltpu.VMEM((orb, orb * pair_rows, LANES), jnp.bfloat16),
            pltpu.VMEM((2, orb, orb * pair_rows, LANES), jnp.bfloat16),
            pltpu.VMEM((orb, 2 * pair_rows, LANES), jnp.float32),
            pltpu.VMEM((tiles, 4, orb, orb, ROWS, LANES), jnp.float32),
            pltpu.VMEM((tiles, 3, orb, orb, ROWS, LANES), jnp.float32),
            pltpu.VMEM((tiles, 3, IBLOCK, orb, ROWS, LANES), jnp.float32),
            pltpu.VMEM((chunks, 2, orb, orb, ext_rows, LANES), jnp.float32),
            pltpu.VMEM((2,) + edge_shape, jnp.float32),
            pltpu.VMEM(halo_shape, jnp.bfloat16),
            pltpu.VMEM(halo_shape, jnp.bfloat16),
            pltpu.VMEM((nz, tile_width, atoms), jnp.bfloat16),
            pltpu.VMEM((nz, chunks, ROWS, LANES), jnp.float32),
            pltpu.VMEM((ne, chunks, ROWS, LANES), jnp.float32),
            pltpu.SMEM((modes,), jnp.float32),
            pltpu.SMEM((modes,), jnp.float32),
            pltpu.SMEM((modes,), jnp.int32),
            pltpu.SMEM((tile_width,), jnp.int32),
            pltpu.VMEM(neighbours.shape, jnp.int32),
            pltpu.VMEM(bond_weight.shape, jnp.bfloat16),
            dma((6,)),
            dma,
            dma,
            dma((chunks, 2, iblocks)),
            dma((chunks, 2, iblocks)),
            dma((nz,)),
            dma((nz,)),
            dma((nz,)),
            dma((nz,)),
            dma((ne,)),
            dma((ne,)),
        ],
        compiler_params=pltpu.CompilerParams(
            collective_id=0, has_side_effects=True, vmem_limit_bytes=64 * 1024 * 1024
        ),
    )(green, broad, coupling, occupation, shifts, bond_count, neighbours, bond_weight)
    out, pol = pl.pallas_call(
        functools.partial(mixing_kernel, orb, energies, atoms),
        grid=(2, 2),
        out_shape=(
            jax.ShapeDtypeStruct((2, orb, orb * pair_rows, atoms), jnp.bfloat16),
            jax.ShapeDtypeStruct((modes // ne, tile_width), jnp.float32),
        ),
        in_specs=[
            pl.BlockSpec((1, chunks, orb // 2, orb * out_rows, LANES), lambda k, ib: (k, 0, ib, 0, 0)),
            pl.BlockSpec((chunks, LANES, atoms), lambda k, ib: (0, 0, 0)),
            pl.BlockSpec((modes // ne, tile_width), lambda k, ib: (0, 0)),
        ],
        out_specs=(
            pl.BlockSpec((1, orb // 2, orb * pair_rows, atoms), lambda k, ib: (k, ib, 0, 0)),
            pl.BlockSpec((modes // ne, tile_width), lambda k, ib: (0, 0)),
        ),
        compiler_params=pltpu.CompilerParams(vmem_limit_bytes=64 * 1024 * 1024),
    )(shifted, mixing, share)
    self_energy = out.reshape(2, orb, orb, energies, 2, atoms).transpose(0, 4, 1, 2, 3, 5)
    return self_energy, pol


def solution(mesh):
    in_specs = (
        P(None, None, None, ("energy", "atom"), None),
        P(None, None, None, None, ("energy", "atom"), None),
        P(),
        P(),
        P(),
        P("atom", None),
        P("atom"),
        P("atom", None),
    )
    out_specs = (P(None, None, None, None, ("energy", "atom"), None), P("energy", "atom"))
    body = functools.partial(local, mesh.shape["energy"], mesh.shape["atom"])
    return jax.shard_map(body, mesh=mesh, in_specs=in_specs, out_specs=out_specs, check_vma=False)
```

```python
import functools
import math

import jax
import jax.numpy as jnp
from jax import lax
from jax.experimental import pallas as pl
from jax.experimental.pallas import tpu as pltpu
from jax.sharding import PartitionSpec as P

SHIFT = 2
LANES = 128
ROWS = 8
IBLOCK = 3
JBLOCK = 4
MESH = pl.DeviceIdType.MESH


def ceil_to(value, step):
    return -(-value // step) * step


def row_plan(energies):
    inner = energies - 2 * SHIFT
    if inner <= 0:
        return [(0, 0, energies), (1, 0, energies)], 2 * energies
    ends = [(k, start, SHIFT) for k in range(2) for start in (0, energies - SHIFT)]
    return ends + [(k, SHIFT, inner) for k in range(2)], 4 * SHIFT


def green_tiles(energies):
    edges, inner = row_plan(energies)[1], energies - 2 * SHIFT
    if inner > 0 and edges % ROWS == 0 and inner % ROWS == 0:
        return edges // ROWS + inner // ROWS
    return pl.cdiv(2 * energies, ROWS)


def pieces(energies):
    parts, place = [], 0
    for k, start, count in row_plan(energies)[0]:
        done = 0
        while done < count:
            tile, row = divmod(place + done, ROWS)
            size = min(ROWS - row, count - done)
            parts.append((tile, row, size, k, start + done))
            done += size
        place += count
    return parts


def keldysh_kernel(
    ne, nz, orb, energies, atoms, modes, slots,
    green, broad, coupling_in, occupation_in, shifts_in, count_in, neighbours_in, weight_in,
    out, share_out,
    gv, sv, plain, gf, sf, hf, ext, edge, send, recv, bonds, mixing, result, first, second,
    mode_rows, mode_shifts, coupling, shifts, count, neighbours, weight, small_sem, out_sem,
    g_sem, s_sem, send_sem, recv_sem, bsend, brecv, fsend, frecv, ssend, srecv,
):
    e = lax.axis_index("energy")
    z = lax.axis_index("atom")
    chunks = atoms // LANES
    pair_rows = 2 * energies
    tiles = pl.cdiv(pair_rows, ROWS)
    edge_tiles = pl.cdiv(row_plan(energies)[1], ROWS)
    repeat = green_tiles(energies)
    halo = 2 * SHIFT
    out_rows = ceil_to(pair_rows, ROWS)
    iblocks, jblocks = orb // IBLOCK, orb // JBLOCK
    tile_width = atoms // nz
    last = ne * nz - 1
    place = e * nz + z

    def at_place(index):
        return {"energy": index // nz, "atom": lax.rem(index, nz)}

    above = at_place(lax.rem(place + 1, ne * nz))
    below = at_place(lax.rem(place + last, ne * nz))

    def input_copies(lc):
        lanes = pl.ds(pl.multiple_of(lc * LANES, LANES), LANES)
        return (
            pltpu.make_async_copy(green.at[:, :, lanes], gv, g_sem),
            pltpu.make_async_copy(broad.at[:, :, :, lanes], sv, s_sem),
        )

    small_copies = [
        pltpu.make_async_copy(source, target, small_sem.at[index])
        for index, (source, target) in enumerate(
            (
                (neighbours_in, neighbours),
                (weight_in, weight),
                (count_in, count),
                (coupling_in, coupling),
                (shifts_in, shifts),
                (coupling_in, mode_rows.at[0]),
                (occupation_in, mode_rows.at[1]),
                (shifts_in, mode_shifts),
            )
        )
    ]
    for copy in small_copies:
        copy.start()
    if chunks == 1:
        for copy in input_copies(0):
            copy.start()

    barrier = pltpu.get_barrier_semaphore()
    pl.semaphore_signal(barrier, inc=1, device_id=above, device_id_type=MESH)
    pl.semaphore_signal(barrier, inc=1, device_id=below, device_id_type=MESH)

    @pl.loop(1, nz)
    def _(step):
        target = {"energy": e, "atom": lax.rem(z + step, nz)}
        pl.semaphore_signal(barrier, inc=1, device_id=target, device_id_type=MESH)

    @pl.loop(1, ne)
    def _(step):
        target = {"energy": lax.rem(e + step, ne), "atom": z}
        pl.semaphore_signal(barrier, inc=1, device_id=target, device_id_type=MESH)

    for copy in small_copies:
        copy.wait()

    row_id = lax.broadcasted_iota(jnp.int32, (tile_width, slots), 0)
    slot_id = lax.broadcasted_iota(jnp.int32, (tile_width, slots), 1)
    live = jnp.zeros((tile_width, slots), jnp.int32)
    for row in range(tile_width):
        live = jnp.where(row_id == row, count[row], live)
    live_weight = jnp.where(slot_id < live, weight[...].astype(jnp.float32), 0.0)
    named = neighbours[...]
    atom_id = lax.broadcasted_iota(jnp.int32, (tile_width, atoms), 1)
    bond_rows = jnp.zeros((tile_width, atoms), jnp.float32)
    for slot in range(slots):
        bond_rows += jnp.where(
            named[:, slot : slot + 1] == atom_id, live_weight[:, slot : slot + 1], 0.0
        )
    bonds[z] = bond_rows.astype(jnp.bfloat16)

    strength, filling, level_of = mode_rows[0], mode_rows[1], mode_shifts[...]
    rounded = []
    for level in range(1, SHIFT + 1):
        for factor in (strength * (filling + 1.0), strength * filling):
            total = jnp.sum(jnp.where(level_of == level, factor, 0.0), axis=1, keepdims=True)
            total = total.astype(jnp.bfloat16).astype(jnp.float32)
            rounded.append(jnp.broadcast_to(total, (out_rows, LANES)))
    emission, absorption = rounded[::2], rounded[1::2]

    def bond_copy(step):
        return pltpu.make_async_remote_copy(
            src_ref=bonds.at[z],
            dst_ref=bonds.at[z],
            send_sem=bsend.at[step],
            recv_sem=brecv.at[step],
            device_id={"energy": e, "atom": lax.rem(z + step, nz)},
            device_id_type=MESH,
        )

    def halo_copy(lc, ib, side):
        return pltpu.make_async_remote_copy(
            src_ref=send.at[lc, side, ib],
            dst_ref=recv.at[lc, side, ib],
            send_sem=send_sem.at[lc, side, ib],
            recv_sem=recv_sem.at[lc, side, ib],
            device_id=above if side else below,
            device_id_type=MESH,
        )

    def green_tile(tile):
        return jnp.where(tile >= repeat, tile - (repeat - edge_tiles), tile)

    def store_forms(target, index, count_of):
        for tile in range(target.shape[0]):
            low = tile * ROWS
            size = min(ROWS, pair_rows - low)
            real = plain[:, pl.ds(2 * low, size, stride=2)]
            imag = plain[:, pl.ds(2 * low + 1, size, stride=2)]
            forms = (real, imag, real + imag, real - imag)
            for form in range(count_of):
                target[tile, form, index, :, 0:size] = forms[form]

    def spread(blocks, limit):
        begin = 0
        for k, start, size in row_plan(energies)[0]:
            if begin < 2 * limit:
                plain[:, begin : begin + 2 * size] = blocks[k][:, 2 * start : 2 * (start + size)]
            begin += 2 * size

    def prepare(lc):
        g_copy, s_copy = input_copies(lc)
        if chunks > 1:
            g_copy.start()
            s_copy.start()
        g_copy.wait()

        @pl.loop(0, orb)
        def _(i):
            block = gv[i].astype(jnp.float32).reshape(orb, pair_rows, LANES)
            spread((block, block), repeat * ROWS)
            store_forms(gf, i, 4)

        s_copy.wait()

        @pl.loop(0, orb)
        def _(i):
            spread(
                [sv[k, i].astype(jnp.float32).reshape(orb, pair_rows, LANES) for k in range(2)],
                pair_rows,
            )
            store_forms(sf, i, 3)

    def keldysh_chunk(lc):
        if chunks > 1:
            prepare(lc)

        def products(ib, first_tile, last_tile):
            irows = pl.ds(ib * IBLOCK, IBLOCK)

            @pl.loop(0, (last_tile - first_tile) * jblocks)
            def _(step):
                tile, jb = first_tile + step // jblocks, lax.rem(step, jblocks)
                jrows = pl.ds(jb * JBLOCK, JBLOCK)
                source = green_tile(tile)
                total = [None] * 3
                for inner in range(orb):
                    for form in range(3):
                        term = gf[source, form, irows, inner][:, None] * sf[tile, form, inner, jrows][None]
                        total[form] = term if inner == 0 else total[form] + term
                real = total[0] - total[1]
                imag = total[2] - total[0] - total[1]
                for form, value in enumerate((real, imag, real + imag)):
                    hf[tile, form, :, jrows] = value

            @pl.loop(0, jblocks)
            def _(jb):
                jrows = pl.ds(jb * JBLOCK, JBLOCK)
                for tile in range(first_tile, last_tile):
                    source = tile if tile < repeat else tile - (repeat - edge_tiles)
                    total = [None] * 3
                    for inner in range(orb):
                        for form, other in enumerate((0, 1, 3)):
                            term = hf[tile, form, :, inner][:, None] * gf[source, other, jrows, inner][None]
                            total[form] = term if inner == 0 else total[form] + term
                    parts = (total[0] + total[1], total[2] - total[0] + total[1])
                    for c, value in enumerate(parts):
                        for t, row, size, k, energy in pieces(energies):
                            if t == tile:
                                start = halo + 2 * energy + c
                                ext[lc, k, irows, jrows, pl.ds(start, size, stride=2)] = value[
                                    :, :, row : row + size
                                ]

        @pl.loop(0, iblocks)
        def _(ib):
            irows = pl.ds(ib * IBLOCK, IBLOCK)
            products(ib, 0, edge_tiles)
            for side, start in enumerate((halo, pair_rows)):
                for k in range(2):
                    for j in range(orb):
                        row = (j % JBLOCK) * halo
                        edge[side, k, :, j // JBLOCK, row : row + halo] = ext[
                            lc, k, irows, j, start : start + halo
                        ]
                send[lc, side, ib] = edge[side].astype(jnp.bfloat16)
                halo_copy(lc, ib, side).start()

        if edge_tiles < tiles:
            @pl.loop(0, iblocks)
            def _(ib):
                products(ib, edge_tiles, tiles)

    if chunks == 1:
        prepare(0)
    pl.semaphore_wait(barrier, 2 + (nz - 1) + (ne - 1))

    @pl.loop(1, nz)
    def _(step):
        bond_copy(step).start()

    if chunks == 1:
        keldysh_chunk(0)
    else:
        pl.loop(0, chunks)(keldysh_chunk)

    def inner_traces(lc):
        def add_row(i, totals):
            result = []
            for offset, total in enumerate(totals, 1):
                size = pair_rows - 2 * offset
                ahead = ext[lc, 0, i, :, halo + 2 * offset : halo + pair_rows]
                behind = ext[lc, 1, :, i, halo : halo + size]
                result.append(total + jnp.sum(ahead * behind, axis=0))
            return tuple(result)

        starts = tuple(
            jnp.zeros((pair_rows - 2 * offset, LANES), jnp.float32)
            for offset in range(1, SHIFT + 1)
        )
        return lax.fori_loop(0, orb, add_row, starts)

    def signed_sum(total):
        parity = lax.rem(lax.broadcasted_iota(jnp.int32, total.shape, 0), 2)
        return jnp.sum(jnp.where(parity == 0, total, -total), axis=0, keepdims=True)

    def store_inner(lc):
        first[0, lc] = jnp.zeros((ROWS, LANES), jnp.float32)
        for offset, total in enumerate(inner_traces(lc)):
            if total.shape[0]:
                first[0, lc, offset : offset + 1] = signed_sum(total)

    if chunks == 1:
        store_inner(0)
    else:
        pl.loop(0, chunks)(store_inner)

    @pl.loop(1, nz)
    def _(step):
        bond_copy(step).wait()

    for lc in range(chunks):
        block = bonds[:, :, lc * LANES : (lc + 1) * LANES].reshape(atoms, LANES)
        mixing[lc] = block.astype(jnp.float32).T.astype(jnp.bfloat16)

    keep_high = (place != last).astype(jnp.float32)
    keep_low = (place != 0).astype(jnp.float32)

    def halo_rows(lc):
        def take_block(ib, totals):
            for side in range(2):
                halo_copy(lc, ib, side).wait()
            irows = pl.ds(ib * IBLOCK, IBLOCK)
            for side, keep in enumerate((keep_high, keep_low)):
                start = 0 if side else halo + pair_rows
                for k in range(2):
                    rows = recv[lc, side, ib, k].astype(jnp.float32) * keep
                    for j in range(orb):
                        row = (j % JBLOCK) * halo
                        ext[lc, k, irows, j, start : start + halo] = rows[
                            :, j // JBLOCK, row : row + halo
                        ]
            totals = list(totals)
            for step in range(IBLOCK):
                i = ib * IBLOCK + step
                for offset in range(1, SHIFT + 1):
                    ahead = ext[lc, 0, :, i, halo : halo + 2 * offset]
                    behind = ext[lc, 1, i, :, halo - 2 * offset : halo]
                    totals[offset - 1] += jnp.sum(ahead * behind, axis=0)
            return tuple(totals)

        starts = tuple(
            jnp.zeros((2 * offset, LANES), jnp.float32) for offset in range(1, SHIFT + 1)
        )
        totals = lax.fori_loop(0, iblocks, take_block, starts)
        for offset, total in enumerate(totals):
            first[0, lc, offset : offset + 1] += signed_sum(total)

    if chunks == 1:
        halo_rows(0)
    else:
        pl.loop(0, chunks)(halo_rows)

    def first_copy(step):
        return pltpu.make_async_remote_copy(
            src_ref=first.at[0],
            dst_ref=first.at[step],
            send_sem=fsend.at[step],
            recv_sem=frecv.at[step],
            device_id={"energy": e, "atom": lax.rem(z + step, nz)},
            device_id_type=MESH,
        )

    def second_copy(step):
        return pltpu.make_async_remote_copy(
            src_ref=second.at[0],
            dst_ref=second.at[step],
            send_sem=ssend.at[step],
            recv_sem=srecv.at[step],
            device_id={"energy": lax.rem(e + step, ne), "atom": z},
            device_id_type=MESH,
        )

    def shift_energies(k):
        upward, downward = (emission, absorption) if k == 0 else (absorption, emission)

        @pl.loop(0, orb)
        def _(i):
            mixed = None
            for lc in range(chunks):
                total = None
                for offset in range(1, SHIFT + 1):
                    for sign, factor in ((1, upward[offset - 1]), (-1, downward[offset - 1])):
                        start = halo + 2 * sign * offset
                        term = factor[None] * ext[lc, k, i, :, start : start + out_rows]
                        total = term if total is None else total + term
                flat = total.reshape(orb * out_rows, LANES).astype(jnp.bfloat16)
                product = jnp.dot(flat, mixing[lc], preferred_element_type=jnp.float32)
                mixed = product if mixed is None else mixed + product
            if out_rows != pair_rows:
                mixed = mixed.reshape(orb, out_rows, atoms)[:, :pair_rows]
                mixed = mixed.reshape(orb * pair_rows, atoms)
            result[k, i] = mixed.astype(jnp.bfloat16)

    def out_copy(k):
        return pltpu.make_async_copy(result.at[k], out.at[k], out_sem.at[k])

    @pl.loop(1, nz)
    def _(step):
        first_copy(step).start()

    shift_energies(0)
    out_copy(0).start()

    @pl.loop(1, nz)
    def _(step):
        first_copy(step).wait()

    second[0] = jnp.sum(first[...], axis=0)

    @pl.loop(1, ne)
    def _(step):
        second_copy(step).start()

    shift_energies(1)
    out_copy(1).start()

    @pl.loop(1, ne)
    def _(step):
        second_copy(step).wait()

    summed = jnp.sum(second[...], axis=0)
    own = jnp.zeros((ROWS, tile_width), jnp.float32)
    for tile in range(nz):
        lc, lane = divmod(tile * tile_width, LANES)
        own = jnp.where(z == tile, summed[lc, :, lane : lane + tile_width], own)
    share = modes // ne
    scale = 1.0 / math.sqrt(energies * ne * nz)
    for row in range(share):
        mode = e * share + row
        shift = shifts[0, mode]
        line = jnp.zeros((1, tile_width), jnp.float32)
        for level in range(1, SHIFT + 1):
            line += jnp.where(shift == level, 1.0, 0.0) * own[level - 1 : level]
        share_out[row : row + 1] = line * (coupling[0, mode] * scale)
    for k in range(2):
        out_copy(k).wait()


def local(ne, nz, green_ret, broadening, coupling, occupation, shifts, neighbours, bond_count, bond_weight):
    orb, energies, atoms = green_ret.shape[1], green_ret.shape[3], green_ret.shape[4]
    modes, slots = coupling.shape[0], neighbours.shape[1]
    tile_width = neighbours.shape[0]
    chunks = atoms // LANES
    pair_rows = 2 * energies
    tiles = pl.cdiv(pair_rows, ROWS)
    out_rows = ceil_to(pair_rows, ROWS)
    ext_rows = ceil_to(max(pair_rows, out_rows) + 4 * SHIFT, ROWS)
    iblocks, jblocks = orb // IBLOCK, orb // JBLOCK
    edge_shape = (2, IBLOCK, jblocks, JBLOCK * 2 * SHIFT, LANES)
    halo_shape = (chunks, 2, iblocks) + edge_shape
    dma = pltpu.SemaphoreType.DMA
    vmem = pl.BlockSpec(memory_space=pltpu.VMEM)
    hbm = pl.BlockSpec(memory_space=pltpu.HBM)
    green = green_ret.transpose(1, 2, 3, 0, 4).reshape(orb, orb * pair_rows, atoms)
    broad = broadening.transpose(0, 2, 3, 4, 1, 5).reshape(2, orb, orb * pair_rows, atoms)
    out, pol = pl.pallas_call(
        functools.partial(keldysh_kernel, ne, nz, orb, energies, atoms, modes, slots),
        out_shape=(
            jax.ShapeDtypeStruct((2, orb, orb * pair_rows, atoms), jnp.bfloat16),
            jax.ShapeDtypeStruct((modes // ne, tile_width), jnp.float32),
        ),
        in_specs=[hbm] * 8,
        out_specs=(hbm, vmem),
        scratch_shapes=[
            pltpu.VMEM((orb, orb * pair_rows, LANES), jnp.bfloat16),
            pltpu.VMEM((2, orb, orb * pair_rows, LANES), jnp.bfloat16),
            pltpu.VMEM((orb, 2 * pair_rows, LANES), jnp.float32),
            pltpu.VMEM((green_tiles(energies), 4, orb, orb, ROWS, LANES), jnp.float32),
            pltpu.VMEM((tiles, 3, orb, orb, ROWS, LANES), jnp.float32),
            pltpu.VMEM((tiles, 3, IBLOCK, orb, ROWS, LANES), jnp.float32),
            pltpu.VMEM((chunks, 2, orb, orb, ext_rows, LANES), jnp.float32),
            pltpu.VMEM((2,) + edge_shape, jnp.float32),
            pltpu.VMEM(halo_shape, jnp.bfloat16),
            pltpu.VMEM(halo_shape, jnp.bfloat16),
            pltpu.VMEM((nz, tile_width, atoms), jnp.bfloat16),
            pltpu.VMEM((chunks, LANES, atoms), jnp.bfloat16),
            pltpu.VMEM((2, orb, orb * pair_rows, atoms), jnp.bfloat16),
            pltpu.VMEM((nz, chunks, ROWS, LANES), jnp.float32),
            pltpu.VMEM((ne, chunks, ROWS, LANES), jnp.float32),
            pltpu.VMEM((2, 1, modes), jnp.float32),
            pltpu.VMEM((1, modes), jnp.int32),
            pltpu.SMEM((1, modes), jnp.float32),
            pltpu.SMEM((1, modes), jnp.int32),
            pltpu.SMEM((tile_width,), jnp.int32),
            pltpu.VMEM(neighbours.shape, jnp.int32),
            pltpu.VMEM(bond_weight.shape, jnp.bfloat16),
            dma((8,)),
            dma((2,)),
            dma,
            dma,
            dma((chunks, 2, iblocks)),
            dma((chunks, 2, iblocks)),
            dma((nz,)),
            dma((nz,)),
            dma((nz,)),
            dma((nz,)),
            dma((ne,)),
            dma((ne,)),
        ],
        compiler_params=pltpu.CompilerParams(
            collective_id=0, has_side_effects=True, vmem_limit_bytes=64 * 1024 * 1024
        ),
    )(
        green,
        broad,
        coupling.reshape(1, modes),
        occupation.reshape(1, modes),
        shifts.reshape(1, modes),
        bond_count,
        neighbours,
        bond_weight,
    )
    self_energy = out.reshape(2, orb, orb, energies, 2, atoms).transpose(0, 4, 1, 2, 3, 5)
    return self_energy, pol


def solution(mesh):
    in_specs = (
        P(None, None, None, ("energy", "atom"), None),
        P(None, None, None, None, ("energy", "atom"), None),
        P(),
        P(),
        P(),
        P("atom", None),
        P("atom"),
        P("atom", None),
    )
    out_specs = (P(None, None, None, None, ("energy", "atom"), None), P("energy", "atom"))
    body = functools.partial(local, mesh.shape["energy"], mesh.shape["atom"])
    return jax.shard_map(body, mesh=mesh, in_specs=in_specs, out_specs=out_specs, check_vma=False)
```

```python
import functools
import math

import jax
import jax.numpy as jnp
from jax import lax
from jax.experimental import pallas as pl
from jax.experimental.pallas import tpu as pltpu
from jax.sharding import PartitionSpec as P

SHIFT = 2
LANES = 128
ROWS = 8
IBLOCK = 6
JBLOCK = 6
PACK = 4
MESH = pl.DeviceIdType.MESH


def ceil_to(value, step):
    return -(-value // step) * step


def row_plan(energies):
    inner = energies - 2 * SHIFT
    if inner <= 0:
        return [(0, 0, energies), (1, 0, energies)], 2 * energies
    ends = [(k, start, SHIFT) for k in range(2) for start in (0, energies - SHIFT)]
    return ends + [(k, SHIFT, inner) for k in range(2)], 4 * SHIFT


def green_tiles(energies):
    edges, inner = row_plan(energies)[1], energies - 2 * SHIFT
    if inner > 0 and edges % ROWS == 0 and inner % ROWS == 0:
        return edges // ROWS + inner // ROWS
    return pl.cdiv(2 * energies, ROWS)


def pieces(energies):
    parts, place = [], 0
    for k, start, count in row_plan(energies)[0]:
        done = 0
        while done < count:
            tile, row = divmod(place + done, ROWS)
            size = min(ROWS - row, count - done)
            parts.append((tile, row, size, k, start + done))
            done += size
        place += count
    return parts


def keldysh_kernel(
    ne, nz, orb, energies, atoms, modes, slots,
    green, broad, coupling_in, occupation_in, shifts_in, count_in, neighbours_in, weight_in,
    out, share_out,
    gv, sv, plain, gf, sf, part, hf, ext, edge, send, recv, bonds, mixing, result, first, second,
    mode_rows, mode_shifts, coupling, shifts, count, neighbours, weight, small_sem, out_sem,
    g_sem, s_sem, send_sem, recv_sem, bsend, brecv, fsend, frecv, ssend, srecv,
):
    e = lax.axis_index("energy")
    z = lax.axis_index("atom")
    chunks = atoms // LANES
    pair_rows = 2 * energies
    tiles = pl.cdiv(pair_rows, ROWS)
    edge_tiles = pl.cdiv(row_plan(energies)[1], ROWS)
    repeat = green_tiles(energies)
    halo = 2 * SHIFT
    out_rows = ceil_to(pair_rows, ROWS)
    iblocks, jblocks = orb // IBLOCK, orb // JBLOCK
    tile_width = atoms // nz
    last = ne * nz - 1
    place = e * nz + z

    def at_place(index):
        return {"energy": index // nz, "atom": lax.rem(index, nz)}

    above = at_place(lax.rem(place + 1, ne * nz))
    below = at_place(lax.rem(place + last, ne * nz))

    def input_copies(lc):
        lanes = pl.ds(pl.multiple_of(lc * LANES, LANES), LANES)
        return (
            pltpu.make_async_copy(green.at[:, :, lanes], gv, g_sem),
            pltpu.make_async_copy(broad.at[:, :, :, lanes], sv, s_sem),
        )

    small_copies = [
        pltpu.make_async_copy(source, target, small_sem.at[index])
        for index, (source, target) in enumerate(
            (
                (neighbours_in, neighbours),
                (weight_in, weight),
                (count_in, count),
                (coupling_in, coupling),
                (shifts_in, shifts),
                (coupling_in, mode_rows.at[0]),
                (occupation_in, mode_rows.at[1]),
                (shifts_in, mode_shifts),
            )
        )
    ]
    for copy in small_copies:
        copy.start()
    if chunks == 1:
        for copy in input_copies(0):
            copy.start()

    barrier = pltpu.get_barrier_semaphore()
    pl.semaphore_signal(barrier, inc=1, device_id=above, device_id_type=MESH)
    pl.semaphore_signal(barrier, inc=1, device_id=below, device_id_type=MESH)

    @pl.loop(1, nz)
    def _(step):
        target = {"energy": e, "atom": lax.rem(z + step, nz)}
        pl.semaphore_signal(barrier, inc=1, device_id=target, device_id_type=MESH)

    @pl.loop(1, ne)
    def _(step):
        target = {"energy": lax.rem(e + step, ne), "atom": z}
        pl.semaphore_signal(barrier, inc=1, device_id=target, device_id_type=MESH)

    for copy in small_copies:
        copy.wait()

    row_id = lax.broadcasted_iota(jnp.int32, (tile_width, slots), 0)
    slot_id = lax.broadcasted_iota(jnp.int32, (tile_width, slots), 1)
    live = jnp.zeros((tile_width, slots), jnp.int32)
    for row in range(tile_width):
        live = jnp.where(row_id == row, count[row], live)
    live_weight = jnp.where(slot_id < live, weight[...].astype(jnp.float32), 0.0)
    named = neighbours[...]
    atom_id = lax.broadcasted_iota(jnp.int32, (tile_width, atoms), 1)
    bond_rows = jnp.zeros((tile_width, atoms), jnp.float32)
    for slot in range(slots):
        bond_rows += jnp.where(
            named[:, slot : slot + 1] == atom_id, live_weight[:, slot : slot + 1], 0.0
        )
    bonds[z] = bond_rows.astype(jnp.bfloat16)

    strength, filling, level_of = mode_rows[0], mode_rows[1], mode_shifts[...]
    rounded = []
    for level in range(1, SHIFT + 1):
        for factor in (strength * (filling + 1.0), strength * filling):
            total = jnp.sum(jnp.where(level_of == level, factor, 0.0), axis=1, keepdims=True)
            total = total.astype(jnp.bfloat16).astype(jnp.float32)
            rounded.append(jnp.broadcast_to(total, (out_rows, LANES)))
    emission, absorption = rounded[::2], rounded[1::2]

    def bond_copy(step):
        return pltpu.make_async_remote_copy(
            src_ref=bonds.at[z],
            dst_ref=bonds.at[z],
            send_sem=bsend.at[step],
            recv_sem=brecv.at[step],
            device_id={"energy": e, "atom": lax.rem(z + step, nz)},
            device_id_type=MESH,
        )

    def halo_copy(lc, ib, side):
        return pltpu.make_async_remote_copy(
            src_ref=send.at[lc, side, ib],
            dst_ref=recv.at[lc, side, ib],
            send_sem=send_sem.at[lc, side, ib],
            recv_sem=recv_sem.at[lc, side, ib],
            device_id=above if side else below,
            device_id_type=MESH,
        )

    def green_tile(tile):
        return jnp.where(tile >= repeat, tile - (repeat - edge_tiles), tile)

    def store_forms(target, index, count_of):
        for tile in range(target.shape[0]):
            low = tile * ROWS
            size = min(ROWS, pair_rows - low)
            real = plain[:, pl.ds(2 * low, size, stride=2)]
            imag = plain[:, pl.ds(2 * low + 1, size, stride=2)]
            forms = (real, imag, real + imag, real - imag)
            for form in range(count_of):
                target[tile, form, index, :, 0:size] = forms[form]

    def spread(blocks, limit):
        begin = 0
        for k, start, size in row_plan(energies)[0]:
            if begin < 2 * limit:
                plain[:, begin : begin + 2 * size] = blocks[k][:, 2 * start : 2 * (start + size)]
            begin += 2 * size

    def prepare(lc):
        g_copy, s_copy = input_copies(lc)
        if chunks > 1:
            g_copy.start()
            s_copy.start()
        g_copy.wait()

        @pl.loop(0, orb)
        def _(i):
            block = gv[i].astype(jnp.float32).reshape(orb, pair_rows, LANES)
            spread((block, block), repeat * ROWS)
            store_forms(gf, i, 4)

        s_copy.wait()

        @pl.loop(0, orb)
        def _(i):
            spread(
                [sv[k, i].astype(jnp.float32).reshape(orb, pair_rows, LANES) for k in range(2)],
                pair_rows,
            )
            store_forms(sf, i, 3)

    def keldysh_chunk(lc):
        if chunks > 1:
            prepare(lc)

        def products(ib, first_tile, last_tile):
            irows = pl.ds(ib * IBLOCK, IBLOCK)

            def block_products(pick):
                for form in range(3):
                    total = None
                    for inner in range(orb):
                        one, two = pick(form, inner)
                        term = one[:, None] * two[None]
                        total = term if inner == 0 else total + term
                    part[form] = total

            @pl.loop(0, (last_tile - first_tile) * jblocks)
            def _(step):
                tile, jb = first_tile + step // jblocks, lax.rem(step, jblocks)
                jrows = pl.ds(jb * JBLOCK, JBLOCK)
                source = green_tile(tile)
                block_products(
                    lambda form, inner: (
                        gf[source, form, irows, inner],
                        sf[tile, form, inner, jrows],
                    )
                )
                for i in range(IBLOCK):
                    one, two, mixed = part[0, i], part[1, i], part[2, i]
                    real = one - two
                    imag = mixed - one - two
                    for form, value in enumerate((real, imag, real + imag)):
                        hf[tile, form, i, jrows] = value

            @pl.loop(0, jblocks)
            def _(jb):
                jrows = pl.ds(jb * JBLOCK, JBLOCK)
                for tile in range(first_tile, last_tile):
                    source = tile if tile < repeat else tile - (repeat - edge_tiles)
                    block_products(
                        lambda form, inner: (
                            hf[tile, form, :, inner],
                            gf[source, (0, 1, 3)[form], jrows, inner],
                        )
                    )
                    one, two, mixed = part[0], part[1], part[2]
                    parts = (one + two, mixed - one + two)
                    for c, value in enumerate(parts):
                        for t, row, size, k, energy in pieces(energies):
                            if t == tile:
                                start = halo + 2 * energy + c
                                ext[lc, k, irows, jrows, pl.ds(start, size, stride=2)] = value[
                                    :, :, row : row + size
                                ]

        @pl.loop(0, iblocks)
        def _(ib):
            irows = pl.ds(ib * IBLOCK, IBLOCK)
            products(ib, 0, edge_tiles)
            for side, start in enumerate((halo, pair_rows)):
                for k in range(2):
                    for j in range(orb):
                        row = (j % PACK) * halo
                        edge[side, k, :, j // PACK, row : row + halo] = ext[
                            lc, k, irows, j, start : start + halo
                        ]
                send[lc, side, ib] = edge[side].astype(jnp.bfloat16)
                halo_copy(lc, ib, side).start()

        if edge_tiles < tiles:
            @pl.loop(0, iblocks)
            def _(ib):
                products(ib, edge_tiles, tiles)

    if chunks == 1:
        prepare(0)
    pl.semaphore_wait(barrier, 2 + (nz - 1) + (ne - 1))

    @pl.loop(1, nz)
    def _(step):
        bond_copy(step).start()

    if chunks == 1:
        keldysh_chunk(0)
    else:
        pl.loop(0, chunks)(keldysh_chunk)

    def inner_traces(lc):
        def add_row(i, totals):
            result = []
            for offset, total in enumerate(totals, 1):
                size = pair_rows - 2 * offset
                ahead = ext[lc, 0, i, :, halo + 2 * offset : halo + pair_rows]
                behind = ext[lc, 1, :, i, halo : halo + size]
                result.append(total + jnp.sum(ahead * behind, axis=0))
            return tuple(result)

        starts = tuple(
            jnp.zeros((pair_rows - 2 * offset, LANES), jnp.float32)
            for offset in range(1, SHIFT + 1)
        )
        return lax.fori_loop(0, orb, add_row, starts)

    def signed_sum(total):
        parity = lax.rem(lax.broadcasted_iota(jnp.int32, total.shape, 0), 2)
        return jnp.sum(jnp.where(parity == 0, total, -total), axis=0, keepdims=True)

    def store_inner(lc):
        first[0, lc] = jnp.zeros((ROWS, LANES), jnp.float32)
        for offset, total in enumerate(inner_traces(lc)):
            if total.shape[0]:
                first[0, lc, offset : offset + 1] = signed_sum(total)

    if chunks == 1:
        store_inner(0)
    else:
        pl.loop(0, chunks)(store_inner)

    @pl.loop(1, nz)
    def _(step):
        bond_copy(step).wait()

    for lc in range(chunks):
        block = bonds[:, :, lc * LANES : (lc + 1) * LANES].reshape(atoms, LANES)
        mixing[lc] = block.astype(jnp.float32).T.astype(jnp.bfloat16)

    keep_high = (place != last).astype(jnp.float32)
    keep_low = (place != 0).astype(jnp.float32)

    def halo_rows(lc):
        def take_block(ib, totals):
            for side in range(2):
                halo_copy(lc, ib, side).wait()
            irows = pl.ds(ib * IBLOCK, IBLOCK)
            for side, keep in enumerate((keep_high, keep_low)):
                start = 0 if side else halo + pair_rows
                for k in range(2):
                    rows = recv[lc, side, ib, k].astype(jnp.float32) * keep
                    for j in range(orb):
                        row = (j % PACK) * halo
                        ext[lc, k, irows, j, start : start + halo] = rows[
                            :, j // PACK, row : row + halo
                        ]
            totals = list(totals)
            for step in range(IBLOCK):
                i = ib * IBLOCK + step
                for offset in range(1, SHIFT + 1):
                    ahead = ext[lc, 0, :, i, halo : halo + 2 * offset]
                    behind = ext[lc, 1, i, :, halo - 2 * offset : halo]
                    totals[offset - 1] += jnp.sum(ahead * behind, axis=0)
            return tuple(totals)

        starts = tuple(
            jnp.zeros((2 * offset, LANES), jnp.float32) for offset in range(1, SHIFT + 1)
        )
        totals = lax.fori_loop(0, iblocks, take_block, starts)
        for offset, total in enumerate(totals):
            first[0, lc, offset : offset + 1] += signed_sum(total)

    if chunks == 1:
        halo_rows(0)
    else:
        pl.loop(0, chunks)(halo_rows)

    def first_copy(step):
        return pltpu.make_async_remote_copy(
            src_ref=first.at[0],
            dst_ref=first.at[step],
            send_sem=fsend.at[step],
            recv_sem=frecv.at[step],
            device_id={"energy": e, "atom": lax.rem(z + step, nz)},
            device_id_type=MESH,
        )

    def second_copy(step):
        return pltpu.make_async_remote_copy(
            src_ref=second.at[0],
            dst_ref=second.at[step],
            send_sem=ssend.at[step],
            recv_sem=srecv.at[step],
            device_id={"energy": lax.rem(e + step, ne), "atom": z},
            device_id_type=MESH,
        )

    def shift_energies(k):
        upward, downward = (emission, absorption) if k == 0 else (absorption, emission)

        @pl.loop(0, orb)
        def _(i):
            mixed = None
            for lc in range(chunks):
                total = None
                for offset in range(1, SHIFT + 1):
                    for sign, factor in ((1, upward[offset - 1]), (-1, downward[offset - 1])):
                        start = halo + 2 * sign * offset
                        term = factor[None] * ext[lc, k, i, :, start : start + out_rows]
                        total = term if total is None else total + term
                flat = total.reshape(orb * out_rows, LANES).astype(jnp.bfloat16)
                product = jnp.dot(flat, mixing[lc], preferred_element_type=jnp.float32)
                mixed = product if mixed is None else mixed + product
            if out_rows != pair_rows:
                mixed = mixed.reshape(orb, out_rows, atoms)[:, :pair_rows]
                mixed = mixed.reshape(orb * pair_rows, atoms)
            result[k, i] = mixed.astype(jnp.bfloat16)

    def out_copy(k):
        return pltpu.make_async_copy(result.at[k], out.at[k], out_sem.at[k])

    @pl.loop(1, nz)
    def _(step):
        first_copy(step).start()

    shift_energies(0)
    out_copy(0).start()

    @pl.loop(1, nz)
    def _(step):
        first_copy(step).wait()

    second[0] = jnp.sum(first[...], axis=0)

    @pl.loop(1, ne)
    def _(step):
        second_copy(step).start()

    shift_energies(1)
    out_copy(1).start()

    @pl.loop(1, ne)
    def _(step):
        second_copy(step).wait()

    summed = jnp.sum(second[...], axis=0)
    own = jnp.zeros((ROWS, tile_width), jnp.float32)
    for tile in range(nz):
        lc, lane = divmod(tile * tile_width, LANES)
        own = jnp.where(z == tile, summed[lc, :, lane : lane + tile_width], own)
    share = modes // ne
    scale = 1.0 / math.sqrt(energies * ne * nz)
    for row in range(share):
        mode = e * share + row
        shift = shifts[0, mode]
        line = jnp.zeros((1, tile_width), jnp.float32)
        for level in range(1, SHIFT + 1):
            line += jnp.where(shift == level, 1.0, 0.0) * own[level - 1 : level]
        share_out[row : row + 1] = line * (coupling[0, mode] * scale)
    for k in range(2):
        out_copy(k).wait()


def copy_kernel(source, small_source, target, small_target, sems):
    half = source.shape[1] // 2
    copies = [pltpu.make_async_copy(small_source, small_target, sems.at[4])]
    for k in range(2):
        for part in range(2):
            rows = pl.ds(part * half, half)
            copies.append(
                pltpu.make_async_copy(
                    source.at[k, rows], target.at[k, rows], sems.at[2 * k + part]
                )
            )
    for copy in copies:
        copy.start()
    for copy in copies:
        copy.wait()


def local(ne, nz, green_ret, broadening, coupling, occupation, shifts, neighbours, bond_count, bond_weight):
    orb, energies, atoms = green_ret.shape[1], green_ret.shape[3], green_ret.shape[4]
    modes, slots = coupling.shape[0], neighbours.shape[1]
    tile_width = neighbours.shape[0]
    chunks = atoms // LANES
    pair_rows = 2 * energies
    tiles = pl.cdiv(pair_rows, ROWS)
    out_rows = ceil_to(pair_rows, ROWS)
    ext_rows = ceil_to(max(pair_rows, out_rows) + 4 * SHIFT, ROWS)
    iblocks = orb // IBLOCK
    edge_shape = (2, IBLOCK, orb // PACK, PACK * 2 * SHIFT, LANES)
    halo_shape = (chunks, 2, iblocks) + edge_shape
    dma = pltpu.SemaphoreType.DMA
    vmem = pl.BlockSpec(memory_space=pltpu.VMEM)
    hbm = pl.BlockSpec(memory_space=pltpu.HBM)
    green = green_ret.transpose(1, 2, 3, 0, 4).reshape(orb, orb * pair_rows, atoms)
    broad = broadening.transpose(0, 2, 3, 4, 1, 5).reshape(2, orb, orb * pair_rows, atoms)
    out, pol = pl.pallas_call(
        functools.partial(keldysh_kernel, ne, nz, orb, energies, atoms, modes, slots),
        out_shape=(
            jax.ShapeDtypeStruct((2, orb, orb * pair_rows, atoms), jnp.bfloat16),
            jax.ShapeDtypeStruct((modes // ne, tile_width), jnp.float32),
        ),
        in_specs=[hbm] * 8,
        out_specs=(hbm, vmem),
        scratch_shapes=[
            pltpu.VMEM((orb, orb * pair_rows, LANES), jnp.bfloat16),
            pltpu.VMEM((2, orb, orb * pair_rows, LANES), jnp.bfloat16),
            pltpu.VMEM((orb, 2 * pair_rows, LANES), jnp.float32),
            pltpu.VMEM((green_tiles(energies), 4, orb, orb, ROWS, LANES), jnp.float32),
            pltpu.VMEM((tiles, 3, orb, orb, ROWS, LANES), jnp.float32),
            pltpu.VMEM((3, IBLOCK, JBLOCK, ROWS, LANES), jnp.float32),
            pltpu.VMEM((tiles, 3, IBLOCK, orb, ROWS, LANES), jnp.float32),
            pltpu.VMEM((chunks, 2, orb, orb, ext_rows, LANES), jnp.float32),
            pltpu.VMEM((2,) + edge_shape, jnp.float32),
            pltpu.VMEM(halo_shape, jnp.bfloat16),
            pltpu.VMEM(halo_shape, jnp.bfloat16),
            pltpu.VMEM((nz, tile_width, atoms), jnp.bfloat16),
            pltpu.VMEM((chunks, LANES, atoms), jnp.bfloat16),
            pltpu.VMEM((2, orb, orb * pair_rows, atoms), jnp.bfloat16),
            pltpu.VMEM((nz, chunks, ROWS, LANES), jnp.float32),
            pltpu.VMEM((ne, chunks, ROWS, LANES), jnp.float32),
            pltpu.VMEM((2, 1, modes), jnp.float32),
            pltpu.VMEM((1, modes), jnp.int32),
            pltpu.SMEM((1, modes), jnp.float32),
            pltpu.SMEM((1, modes), jnp.int32),
            pltpu.SMEM((tile_width,), jnp.int32),
            pltpu.VMEM(neighbours.shape, jnp.int32),
            pltpu.VMEM(bond_weight.shape, jnp.bfloat16),
            dma((8,)),
            dma((2,)),
            dma,
            dma,
            dma((chunks, 2, iblocks)),
            dma((chunks, 2, iblocks)),
            dma((nz,)),
            dma((nz,)),
            dma((nz,)),
            dma((nz,)),
            dma((ne,)),
            dma((ne,)),
        ],
        compiler_params=pltpu.CompilerParams(
            collective_id=0, has_side_effects=True, vmem_limit_bytes=64 * 1024 * 1024
        ),
    )(
        green,
        broad,
        coupling.reshape(1, modes),
        occupation.reshape(1, modes),
        shifts.reshape(1, modes),
        bond_count,
        neighbours,
        bond_weight,
    )
    out, pol = pl.pallas_call(
        copy_kernel,
        out_shape=(
            jax.ShapeDtypeStruct(out.shape, out.dtype),
            jax.ShapeDtypeStruct(pol.shape, pol.dtype),
        ),
        in_specs=[hbm] * 2,
        out_specs=(hbm, hbm),
        scratch_shapes=[dma((5,))],
        compiler_params=pltpu.CompilerParams(vmem_limit_bytes=64 * 1024 * 1024),
    )(out, pol)
    self_energy = out.reshape(2, orb, orb, energies, 2, atoms).transpose(0, 4, 1, 2, 3, 5)
    return self_energy, pol


def solution(mesh):
    in_specs = (
        P(None, None, None, ("energy", "atom"), None),
        P(None, None, None, None, ("energy", "atom"), None),
        P(),
        P(),
        P(),
        P("atom", None),
        P("atom"),
        P("atom", None),
    )
    out_specs = (P(None, None, None, None, ("energy", "atom"), None), P("energy", "atom"))
    body = functools.partial(local, mesh.shape["energy"], mesh.shape["atom"])
    return jax.shard_map(body, mesh=mesh, in_specs=in_specs, out_specs=out_specs, check_vma=False)
```

```python
import functools
import math

import jax
import jax.numpy as jnp
from jax import lax
from jax.experimental import pallas as pl
from jax.experimental.pallas import tpu as pltpu
from jax.sharding import PartitionSpec as P

SHIFT = 2
LANES = 128
ROWS = 8
IBLOCK = 3
JBLOCK = 3
PACK = 4
MESH = pl.DeviceIdType.MESH


def ceil_to(value, step):
    return -(-value // step) * step


def row_plan(energies):
    inner = energies - 2 * SHIFT
    if inner <= 0:
        return [(0, 0, energies), (1, 0, energies)], 2 * energies
    ends = [(k, start, SHIFT) for k in range(2) for start in (0, energies - SHIFT)]
    return ends + [(k, SHIFT, inner) for k in range(2)], 4 * SHIFT


def green_tiles(energies):
    edges, inner = row_plan(energies)[1], energies - 2 * SHIFT
    if inner > 0 and edges % ROWS == 0 and inner % ROWS == 0:
        return edges // ROWS + inner // ROWS
    return pl.cdiv(2 * energies, ROWS)


def pieces(energies):
    parts, place = [], 0
    for k, start, count in row_plan(energies)[0]:
        done = 0
        while done < count:
            tile, row = divmod(place + done, ROWS)
            size = min(ROWS - row, count - done)
            parts.append((tile, row, size, k, start + done))
            done += size
        place += count
    return parts


def keldysh_kernel(
    ne, nz, orb, energies, atoms, modes, slots,
    green, broad, coupling_in, occupation_in, shifts_in, count_in, neighbours_in, weight_in,
    out, share_out,
    gv, sv, plain, gf, sf, hf, ext, edge, send, recv, bonds, mixing, result, first, second,
    mode_rows, mode_shifts, coupling, shifts, count, neighbours, weight, small_sem, out_sem,
    g_sem, s_sem, send_sem, recv_sem, bsend, brecv, fsend, frecv, ssend, srecv,
):
    e = lax.axis_index("energy")
    z = lax.axis_index("atom")
    chunks = atoms // LANES
    pair_rows = 2 * energies
    tiles = pl.cdiv(pair_rows, ROWS)
    edge_tiles = pl.cdiv(row_plan(energies)[1], ROWS)
    repeat = green_tiles(energies)
    halo = 2 * SHIFT
    out_rows = ceil_to(pair_rows, ROWS)
    iblocks, jblocks = orb // IBLOCK, orb // JBLOCK
    tile_width = atoms // nz
    last = ne * nz - 1
    place = e * nz + z

    def at_place(index):
        return {"energy": index // nz, "atom": lax.rem(index, nz)}

    above = at_place(lax.rem(place + 1, ne * nz))
    below = at_place(lax.rem(place + last, ne * nz))

    def input_copies(lc):
        lanes = pl.ds(pl.multiple_of(lc * LANES, LANES), LANES)
        return (
            pltpu.make_async_copy(green.at[:, :, lanes], gv, g_sem),
            pltpu.make_async_copy(broad.at[:, :, :, lanes], sv, s_sem),
        )

    small_copies = [
        pltpu.make_async_copy(source, target, small_sem.at[index])
        for index, (source, target) in enumerate(
            (
                (neighbours_in, neighbours),
                (weight_in, weight),
                (count_in, count),
                (coupling_in, coupling),
                (shifts_in, shifts),
                (coupling_in, mode_rows.at[0]),
                (occupation_in, mode_rows.at[1]),
                (shifts_in, mode_shifts),
            )
        )
    ]
    for copy in small_copies:
        copy.start()
    if chunks == 1:
        for copy in input_copies(0):
            copy.start()

    barrier = pltpu.get_barrier_semaphore()
    pl.semaphore_signal(barrier, inc=1, device_id=above, device_id_type=MESH)
    pl.semaphore_signal(barrier, inc=1, device_id=below, device_id_type=MESH)

    @pl.loop(1, nz)
    def _(step):
        target = {"energy": e, "atom": lax.rem(z + step, nz)}
        pl.semaphore_signal(barrier, inc=1, device_id=target, device_id_type=MESH)

    @pl.loop(1, ne)
    def _(step):
        target = {"energy": lax.rem(e + step, ne), "atom": z}
        pl.semaphore_signal(barrier, inc=1, device_id=target, device_id_type=MESH)

    for copy in small_copies:
        copy.wait()

    row_id = lax.broadcasted_iota(jnp.int32, (tile_width, slots), 0)
    slot_id = lax.broadcasted_iota(jnp.int32, (tile_width, slots), 1)
    live = jnp.zeros((tile_width, slots), jnp.int32)
    for row in range(tile_width):
        live = jnp.where(row_id == row, count[row], live)
    live_weight = jnp.where(slot_id < live, weight[...].astype(jnp.float32), 0.0)
    named = neighbours[...]
    atom_id = lax.broadcasted_iota(jnp.int32, (tile_width, atoms), 1)
    bond_rows = jnp.zeros((tile_width, atoms), jnp.float32)
    for slot in range(slots):
        bond_rows += jnp.where(
            named[:, slot : slot + 1] == atom_id, live_weight[:, slot : slot + 1], 0.0
        )
    bonds[z] = bond_rows.astype(jnp.bfloat16)

    strength, filling, level_of = mode_rows[0], mode_rows[1], mode_shifts[...]
    rounded = []
    for level in range(1, SHIFT + 1):
        for factor in (strength * (filling + 1.0), strength * filling):
            total = jnp.sum(jnp.where(level_of == level, factor, 0.0), axis=1, keepdims=True)
            total = total.astype(jnp.bfloat16).astype(jnp.float32)
            rounded.append(jnp.broadcast_to(total, (out_rows, LANES)))
    emission, absorption = rounded[::2], rounded[1::2]

    def bond_copy(step):
        return pltpu.make_async_remote_copy(
            src_ref=bonds.at[z],
            dst_ref=bonds.at[z],
            send_sem=bsend.at[step],
            recv_sem=brecv.at[step],
            device_id={"energy": e, "atom": lax.rem(z + step, nz)},
            device_id_type=MESH,
        )

    def halo_copy(lc, ib, side):
        return pltpu.make_async_remote_copy(
            src_ref=send.at[lc, side, ib],
            dst_ref=recv.at[lc, side, ib],
            send_sem=send_sem.at[lc, side, ib],
            recv_sem=recv_sem.at[lc, side, ib],
            device_id=above if side else below,
            device_id_type=MESH,
        )

    def green_tile(tile):
        return jnp.where(tile >= repeat, tile - (repeat - edge_tiles), tile)

    def store_forms(target, index, count_of):
        for tile in range(target.shape[0]):
            low = tile * ROWS
            size = min(ROWS, pair_rows - low)
            real = plain[:, pl.ds(2 * low, size, stride=2)]
            imag = plain[:, pl.ds(2 * low + 1, size, stride=2)]
            forms = (real, imag, real + imag, real - imag)
            for form in range(count_of):
                target[tile, form, index, :, 0:size] = forms[form]

    def spread(blocks, limit):
        begin = 0
        for k, start, size in row_plan(energies)[0]:
            if begin < 2 * limit:
                plain[:, begin : begin + 2 * size] = blocks[k][:, 2 * start : 2 * (start + size)]
            begin += 2 * size

    def prepare(lc):
        g_copy, s_copy = input_copies(lc)
        if chunks > 1:
            g_copy.start()
            s_copy.start()
        g_copy.wait()

        @pl.loop(0, orb)
        def _(i):
            block = gv[i].astype(jnp.float32).reshape(orb, pair_rows, LANES)
            spread((block, block), repeat * ROWS)
            store_forms(gf, i, 4)

        s_copy.wait()

        @pl.loop(0, orb)
        def _(i):
            spread(
                [sv[k, i].astype(jnp.float32).reshape(orb, pair_rows, LANES) for k in range(2)],
                pair_rows,
            )
            store_forms(sf, i, 3)

    def keldysh_chunk(lc):
        if chunks > 1:
            prepare(lc)

        def products(ib, first_tile, last_tile):
            irows = pl.ds(ib * IBLOCK, IBLOCK)

            @pl.loop(0, (last_tile - first_tile) * jblocks)
            def _(step):
                tile, jb = first_tile + step // jblocks, lax.rem(step, jblocks)
                jrows = pl.ds(jb * JBLOCK, JBLOCK)
                source = green_tile(tile)
                total = [None] * 3
                for inner in range(orb):
                    for form in range(3):
                        term = gf[source, form, irows, inner][:, None] * sf[tile, form, inner, jrows][None]
                        total[form] = term if inner == 0 else total[form] + term
                real = total[0] - total[1]
                imag = total[2] - total[0] - total[1]
                for form, value in enumerate((real, imag, real + imag)):
                    hf[tile, form, :, jrows] = value

            @pl.loop(0, jblocks)
            def _(jb):
                jrows = pl.ds(jb * JBLOCK, JBLOCK)
                for tile in range(first_tile, last_tile):
                    source = tile if tile < repeat else tile - (repeat - edge_tiles)
                    total = [None] * 3
                    for inner in range(orb):
                        for form, other in enumerate((0, 1, 3)):
                            term = hf[tile, form, :, inner][:, None] * gf[source, other, jrows, inner][None]
                            total[form] = term if inner == 0 else total[form] + term
                    parts = (total[0] + total[1], total[2] - total[0] + total[1])
                    for c, value in enumerate(parts):
                        for t, row, size, k, energy in pieces(energies):
                            if t == tile:
                                start = halo + 2 * energy + c
                                ext[lc, k, irows, jrows, pl.ds(start, size, stride=2)] = value[
                                    :, :, row : row + size
                                ]

        @pl.loop(0, iblocks)
        def _(ib):
            irows = pl.ds(ib * IBLOCK, IBLOCK)
            products(ib, 0, edge_tiles)
            for side, start in enumerate((halo, pair_rows)):
                for k in range(2):
                    for j in range(orb):
                        row = (j % PACK) * halo
                        edge[side, k, :, j // PACK, row : row + halo] = ext[
                            lc, k, irows, j, start : start + halo
                        ]
                send[lc, side, ib] = edge[side].astype(jnp.bfloat16)
                halo_copy(lc, ib, side).start()

        if edge_tiles < tiles:
            @pl.loop(0, iblocks)
            def _(ib):
                products(ib, edge_tiles, tiles)

    if chunks == 1:
        prepare(0)
    pl.semaphore_wait(barrier, 2 + (nz - 1) + (ne - 1))

    @pl.loop(1, nz)
    def _(step):
        bond_copy(step).start()

    if chunks == 1:
        keldysh_chunk(0)
    else:
        pl.loop(0, chunks)(keldysh_chunk)

    def inner_traces(lc):
        def add_row(i, totals):
            result = []
            for offset, total in enumerate(totals, 1):
                size = pair_rows - 2 * offset
                ahead = ext[lc, 0, i, :, halo + 2 * offset : halo + pair_rows]
                behind = ext[lc, 1, :, i, halo : halo + size]
                result.append(total + jnp.sum(ahead * behind, axis=0))
            return tuple(result)

        starts = tuple(
            jnp.zeros((pair_rows - 2 * offset, LANES), jnp.float32)
            for offset in range(1, SHIFT + 1)
        )
        return lax.fori_loop(0, orb, add_row, starts)

    def signed_sum(total):
        parity = lax.rem(lax.broadcasted_iota(jnp.int32, total.shape, 0), 2)
        return jnp.sum(jnp.where(parity == 0, total, -total), axis=0, keepdims=True)

    def store_inner(lc):
        first[0, lc] = jnp.zeros((ROWS, LANES), jnp.float32)
        for offset, total in enumerate(inner_traces(lc)):
            if total.shape[0]:
                first[0, lc, offset : offset + 1] = signed_sum(total)

    if chunks == 1:
        store_inner(0)
    else:
        pl.loop(0, chunks)(store_inner)

    @pl.loop(1, nz)
    def _(step):
        bond_copy(step).wait()

    for lc in range(chunks):
        block = bonds[:, :, lc * LANES : (lc + 1) * LANES].reshape(atoms, LANES)
        mixing[lc] = block.astype(jnp.float32).T.astype(jnp.bfloat16)

    keep_high = (place != last).astype(jnp.float32)
    keep_low = (place != 0).astype(jnp.float32)

    def halo_rows(lc):
        def take_block(ib, totals):
            for side in range(2):
                halo_copy(lc, ib, side).wait()
            irows = pl.ds(ib * IBLOCK, IBLOCK)
            for side, keep in enumerate((keep_high, keep_low)):
                start = 0 if side else halo + pair_rows
                for k in range(2):
                    rows = recv[lc, side, ib, k].astype(jnp.float32) * keep
                    for j in range(orb):
                        row = (j % PACK) * halo
                        ext[lc, k, irows, j, start : start + halo] = rows[
                            :, j // PACK, row : row + halo
                        ]
            totals = list(totals)
            for step in range(IBLOCK):
                i = ib * IBLOCK + step
                for offset in range(1, SHIFT + 1):
                    ahead = ext[lc, 0, :, i, halo : halo + 2 * offset]
                    behind = ext[lc, 1, i, :, halo - 2 * offset : halo]
                    totals[offset - 1] += jnp.sum(ahead * behind, axis=0)
            return tuple(totals)

        starts = tuple(
            jnp.zeros((2 * offset, LANES), jnp.float32) for offset in range(1, SHIFT + 1)
        )
        totals = lax.fori_loop(0, iblocks, take_block, starts)
        for offset, total in enumerate(totals):
            first[0, lc, offset : offset + 1] += signed_sum(total)

    if chunks == 1:
        halo_rows(0)
    else:
        pl.loop(0, chunks)(halo_rows)

    def first_copy(step):
        return pltpu.make_async_remote_copy(
            src_ref=first.at[0],
            dst_ref=first.at[step],
            send_sem=fsend.at[step],
            recv_sem=frecv.at[step],
            device_id={"energy": e, "atom": lax.rem(z + step, nz)},
            device_id_type=MESH,
        )

    def second_copy(step):
        return pltpu.make_async_remote_copy(
            src_ref=second.at[0],
            dst_ref=second.at[step],
            send_sem=ssend.at[step],
            recv_sem=srecv.at[step],
            device_id={"energy": lax.rem(e + step, ne), "atom": z},
            device_id_type=MESH,
        )

    def shift_energies(k):
        upward, downward = (emission, absorption) if k == 0 else (absorption, emission)

        @pl.loop(0, orb)
        def _(i):
            mixed = None
            for lc in range(chunks):
                total = None
                for offset in range(1, SHIFT + 1):
                    for sign, factor in ((1, upward[offset - 1]), (-1, downward[offset - 1])):
                        start = halo + 2 * sign * offset
                        term = factor[None] * ext[lc, k, i, :, start : start + out_rows]
                        total = term if total is None else total + term
                flat = total.reshape(orb * out_rows, LANES).astype(jnp.bfloat16)
                product = jnp.dot(flat, mixing[lc], preferred_element_type=jnp.float32)
                mixed = product if mixed is None else mixed + product
            if out_rows != pair_rows:
                mixed = mixed.reshape(orb, out_rows, atoms)[:, :pair_rows]
                mixed = mixed.reshape(orb * pair_rows, atoms)
            result[k, i] = mixed.astype(jnp.bfloat16)

    def out_copy(k):
        return pltpu.make_async_copy(result.at[k], out.at[k], out_sem.at[k])

    @pl.loop(1, nz)
    def _(step):
        first_copy(step).start()

    shift_energies(0)
    out_copy(0).start()

    @pl.loop(1, nz)
    def _(step):
        first_copy(step).wait()

    second[0] = jnp.sum(first[...], axis=0)

    @pl.loop(1, ne)
    def _(step):
        second_copy(step).start()

    shift_energies(1)
    out_copy(1).start()

    @pl.loop(1, ne)
    def _(step):
        second_copy(step).wait()

    summed = jnp.sum(second[...], axis=0)
    own = jnp.zeros((ROWS, tile_width), jnp.float32)
    for tile in range(nz):
        lc, lane = divmod(tile * tile_width, LANES)
        own = jnp.where(z == tile, summed[lc, :, lane : lane + tile_width], own)
    share = modes // ne
    scale = 1.0 / math.sqrt(energies * ne * nz)
    for row in range(share):
        mode = e * share + row
        shift = shifts[0, mode]
        line = jnp.zeros((1, tile_width), jnp.float32)
        for level in range(1, SHIFT + 1):
            line += jnp.where(shift == level, 1.0, 0.0) * own[level - 1 : level]
        share_out[row : row + 1] = line * (coupling[0, mode] * scale)
    for k in range(2):
        out_copy(k).wait()


def copy_kernel(source, small_source, target, small_target, held, small_held, in_sems, out_sems):
    half = source.shape[1] // 2
    stages = [(small_source, small_held, small_target)]
    for k in range(2):
        for part in range(2):
            rows = pl.ds(part * half, half)
            stages.append((source.at[k, rows], held.at[k, rows], target.at[k, rows]))
    loads = [
        pltpu.make_async_copy(first, middle, in_sems.at[index])
        for index, (first, middle, last) in enumerate(stages)
    ]
    stores = [
        pltpu.make_async_copy(middle, last, out_sems.at[index])
        for index, (first, middle, last) in enumerate(stages)
    ]
    for load in loads:
        load.start()
    for load, store in zip(loads, stores):
        load.wait()
        store.start()
    for store in stores:
        store.wait()


def local(ne, nz, green_ret, broadening, coupling, occupation, shifts, neighbours, bond_count, bond_weight):
    orb, energies, atoms = green_ret.shape[1], green_ret.shape[3], green_ret.shape[4]
    modes, slots = coupling.shape[0], neighbours.shape[1]
    tile_width = neighbours.shape[0]
    chunks = atoms // LANES
    pair_rows = 2 * energies
    tiles = pl.cdiv(pair_rows, ROWS)
    out_rows = ceil_to(pair_rows, ROWS)
    ext_rows = ceil_to(max(pair_rows, out_rows) + 4 * SHIFT, ROWS)
    iblocks = orb // IBLOCK
    edge_shape = (2, IBLOCK, orb // PACK, PACK * 2 * SHIFT, LANES)
    halo_shape = (chunks, 2, iblocks) + edge_shape
    dma = pltpu.SemaphoreType.DMA
    vmem = pl.BlockSpec(memory_space=pltpu.VMEM)
    hbm = pl.BlockSpec(memory_space=pltpu.HBM)
    green = green_ret.transpose(1, 2, 3, 0, 4).reshape(orb, orb * pair_rows, atoms)
    broad = broadening.transpose(0, 2, 3, 4, 1, 5).reshape(2, orb, orb * pair_rows, atoms)
    out, pol = pl.pallas_call(
        functools.partial(keldysh_kernel, ne, nz, orb, energies, atoms, modes, slots),
        out_shape=(
            jax.ShapeDtypeStruct((2, orb, orb * pair_rows, atoms), jnp.bfloat16),
            jax.ShapeDtypeStruct((modes // ne, tile_width), jnp.float32),
        ),
        in_specs=[hbm] * 8,
        out_specs=(hbm, vmem),
        scratch_shapes=[
            pltpu.VMEM((orb, orb * pair_rows, LANES), jnp.bfloat16),
            pltpu.VMEM((2, orb, orb * pair_rows, LANES), jnp.bfloat16),
            pltpu.VMEM((orb, 2 * pair_rows, LANES), jnp.float32),
            pltpu.VMEM((green_tiles(energies), 4, orb, orb, ROWS, LANES), jnp.float32),
            pltpu.VMEM((tiles, 3, orb, orb, ROWS, LANES), jnp.float32),
            pltpu.VMEM((tiles, 3, IBLOCK, orb, ROWS, LANES), jnp.float32),
            pltpu.VMEM((chunks, 2, orb, orb, ext_rows, LANES), jnp.float32),
            pltpu.VMEM((2,) + edge_shape, jnp.float32),
            pltpu.VMEM(halo_shape, jnp.bfloat16),
            pltpu.VMEM(halo_shape, jnp.bfloat16),
            pltpu.VMEM((nz, tile_width, atoms), jnp.bfloat16),
            pltpu.VMEM((chunks, LANES, atoms), jnp.bfloat16),
            pltpu.VMEM((2, orb, orb * pair_rows, atoms), jnp.bfloat16),
            pltpu.VMEM((nz, chunks, ROWS, LANES), jnp.float32),
            pltpu.VMEM((ne, chunks, ROWS, LANES), jnp.float32),
            pltpu.VMEM((2, 1, modes), jnp.float32),
            pltpu.VMEM((1, modes), jnp.int32),
            pltpu.SMEM((1, modes), jnp.float32),
            pltpu.SMEM((1, modes), jnp.int32),
            pltpu.SMEM((tile_width,), jnp.int32),
            pltpu.VMEM(neighbours.shape, jnp.int32),
            pltpu.VMEM(bond_weight.shape, jnp.bfloat16),
            dma((8,)),
            dma((2,)),
            dma,
            dma,
            dma((chunks, 2, iblocks)),
            dma((chunks, 2, iblocks)),
            dma((nz,)),
            dma((nz,)),
            dma((nz,)),
            dma((nz,)),
            dma((ne,)),
            dma((ne,)),
        ],
        compiler_params=pltpu.CompilerParams(
            collective_id=0, has_side_effects=True, vmem_limit_bytes=64 * 1024 * 1024
        ),
    )(
        green,
        broad,
        coupling.reshape(1, modes),
        occupation.reshape(1, modes),
        shifts.reshape(1, modes),
        bond_count,
        neighbours,
        bond_weight,
    )
    out, pol = pl.pallas_call(
        copy_kernel,
        out_shape=(
            jax.ShapeDtypeStruct(out.shape, out.dtype),
            jax.ShapeDtypeStruct(pol.shape, pol.dtype),
        ),
        in_specs=[hbm] * 2,
        out_specs=(hbm, hbm),
        scratch_shapes=[
            pltpu.VMEM(out.shape, out.dtype),
            pltpu.VMEM(pol.shape, pol.dtype),
            dma((5,)),
            dma((5,)),
        ],
        compiler_params=pltpu.CompilerParams(vmem_limit_bytes=64 * 1024 * 1024),
    )(out, pol)
    self_energy = out.reshape(2, orb, orb, energies, 2, atoms).transpose(0, 4, 1, 2, 3, 5)
    return self_energy, pol


def solution(mesh):
    in_specs = (
        P(None, None, None, ("energy", "atom"), None),
        P(None, None, None, None, ("energy", "atom"), None),
        P(),
        P(),
        P(),
        P("atom", None),
        P("atom"),
        P("atom", None),
    )
    out_specs = (P(None, None, None, None, ("energy", "atom"), None), P("energy", "atom"))
    body = functools.partial(local, mesh.shape["energy"], mesh.shape["atom"])
    return jax.shard_map(body, mesh=mesh, in_specs=in_specs, out_specs=out_specs, check_vma=False)
```

```python
import functools
import math

import jax
import jax.numpy as jnp
from jax import lax
from jax.experimental import pallas as pl
from jax.experimental.pallas import tpu as pltpu
from jax.sharding import PartitionSpec as P

SHIFT = 2
LANES = 128
ROWS = 8
IBLOCK = 3
JBLOCK = 3
PACK = 4
MESH = pl.DeviceIdType.MESH


def ceil_to(value, step):
    return -(-value // step) * step


def row_plan(energies):
    inner = energies - 2 * SHIFT
    if inner <= 0:
        return [(0, 0, energies), (1, 0, energies)], 2 * energies
    ends = [(k, start, SHIFT) for k in range(2) for start in (0, energies - SHIFT)]
    return ends + [(k, SHIFT, inner) for k in range(2)], 4 * SHIFT


def green_tiles(energies):
    edges, inner = row_plan(energies)[1], energies - 2 * SHIFT
    if inner > 0 and edges % ROWS == 0 and inner % ROWS == 0:
        return edges // ROWS + inner // ROWS
    return pl.cdiv(2 * energies, ROWS)


def pieces(energies):
    parts, place = [], 0
    for k, start, count in row_plan(energies)[0]:
        done = 0
        while done < count:
            tile, row = divmod(place + done, ROWS)
            size = min(ROWS - row, count - done)
            parts.append((tile, row, size, k, start + done))
            done += size
        place += count
    return parts


def keldysh_kernel(
    ne, nz, orb, energies, atoms, modes, slots,
    green, broad, coupling_in, occupation_in, shifts_in, count_in, neighbours_in, weight_in,
    out, share_out,
    gv, sv, plain, gf, sf, hf, ext, edge, send, recv, bonds, mixing, result, first, second,
    mode_rows, mode_shifts, coupling, shifts, count, neighbours, weight, small_sem, out_sem,
    g_sem, s_sem, send_sem, recv_sem, bsend, brecv, fsend, frecv, ssend, srecv,
):
    e = lax.axis_index("energy")
    z = lax.axis_index("atom")
    chunks = atoms // LANES
    pair_rows = 2 * energies
    tiles = pl.cdiv(pair_rows, ROWS)
    edge_tiles = pl.cdiv(row_plan(energies)[1], ROWS)
    repeat = green_tiles(energies)
    halo = 2 * SHIFT
    out_rows = ceil_to(pair_rows, ROWS)
    iblocks, jblocks = orb // IBLOCK, orb // JBLOCK
    tile_width = atoms // nz
    last = ne * nz - 1
    place = e * nz + z

    def at_place(index):
        return {"energy": index // nz, "atom": lax.rem(index, nz)}

    above = at_place(lax.rem(place + 1, ne * nz))
    below = at_place(lax.rem(place + last, ne * nz))

    def input_copies(lc):
        lanes = pl.ds(pl.multiple_of(lc * LANES, LANES), LANES)
        return (
            pltpu.make_async_copy(green.at[:, :, lanes], gv, g_sem),
            pltpu.make_async_copy(broad.at[:, :, :, lanes], sv, s_sem),
        )

    small_copies = [
        pltpu.make_async_copy(source, target, small_sem.at[index])
        for index, (source, target) in enumerate(
            (
                (neighbours_in, neighbours),
                (weight_in, weight),
                (count_in, count),
                (coupling_in, coupling),
                (shifts_in, shifts),
                (coupling_in, mode_rows.at[0]),
                (occupation_in, mode_rows.at[1]),
                (shifts_in, mode_shifts),
            )
        )
    ]
    for copy in small_copies:
        copy.start()
    if chunks == 1:
        for copy in input_copies(0):
            copy.start()

    barrier = pltpu.get_barrier_semaphore()
    pl.semaphore_signal(barrier, inc=1, device_id=above, device_id_type=MESH)
    pl.semaphore_signal(barrier, inc=1, device_id=below, device_id_type=MESH)

    @pl.loop(1, nz)
    def _(step):
        target = {"energy": e, "atom": lax.rem(z + step, nz)}
        pl.semaphore_signal(barrier, inc=1, device_id=target, device_id_type=MESH)

    @pl.loop(1, ne)
    def _(step):
        target = {"energy": lax.rem(e + step, ne), "atom": z}
        pl.semaphore_signal(barrier, inc=1, device_id=target, device_id_type=MESH)

    for copy in small_copies:
        copy.wait()

    row_id = lax.broadcasted_iota(jnp.int32, (tile_width, slots), 0)
    slot_id = lax.broadcasted_iota(jnp.int32, (tile_width, slots), 1)
    live = jnp.zeros((tile_width, slots), jnp.int32)
    for row in range(tile_width):
        live = jnp.where(row_id == row, count[row], live)
    live_weight = jnp.where(slot_id < live, weight[...].astype(jnp.float32), 0.0)
    named = neighbours[...]
    atom_id = lax.broadcasted_iota(jnp.int32, (tile_width, atoms), 1)
    bond_rows = jnp.zeros((tile_width, atoms), jnp.float32)
    for slot in range(slots):
        bond_rows += jnp.where(
            named[:, slot : slot + 1] == atom_id, live_weight[:, slot : slot + 1], 0.0
        )
    bonds[z] = bond_rows.astype(jnp.bfloat16)

    strength, filling, level_of = mode_rows[0], mode_rows[1], mode_shifts[...]
    rounded = []
    for level in range(1, SHIFT + 1):
        for factor in (strength * (filling + 1.0), strength * filling):
            total = jnp.sum(jnp.where(level_of == level, factor, 0.0), axis=1, keepdims=True)
            total = total.astype(jnp.bfloat16).astype(jnp.float32)
            rounded.append(jnp.broadcast_to(total, (out_rows, LANES)))
    emission, absorption = rounded[::2], rounded[1::2]

    def bond_copy(step):
        return pltpu.make_async_remote_copy(
            src_ref=bonds.at[z],
            dst_ref=bonds.at[z],
            send_sem=bsend.at[step],
            recv_sem=brecv.at[step],
            device_id={"energy": e, "atom": lax.rem(z + step, nz)},
            device_id_type=MESH,
        )

    def halo_copy(lc, ib, side):
        return pltpu.make_async_remote_copy(
            src_ref=send.at[lc, side, ib],
            dst_ref=recv.at[lc, side, ib],
            send_sem=send_sem.at[lc, side, ib],
            recv_sem=recv_sem.at[lc, side, ib],
            device_id=above if side else below,
            device_id_type=MESH,
        )

    def green_tile(tile):
        return jnp.where(tile >= repeat, tile - (repeat - edge_tiles), tile)

    def store_forms(plain, target, index, count_of):
        for tile in range(target.shape[0]):
            low = tile * ROWS
            size = min(ROWS, pair_rows - low)
            real = plain[:, pl.ds(2 * low, size, stride=2)]
            imag = plain[:, pl.ds(2 * low + 1, size, stride=2)]
            forms = (real, imag, real + imag, real - imag)
            for form in range(count_of):
                target[tile, form, index, :, 0:size] = forms[form]

    def spread(plain, blocks, limit):
        begin = 0
        for k, start, size in row_plan(energies)[0]:
            if begin < 2 * limit:
                plain[:, begin : begin + 2 * size] = blocks[k][:, 2 * start : 2 * (start + size)]
            begin += 2 * size

    def prepare(lc):
        g_copy, s_copy = input_copies(lc)
        if chunks > 1:
            g_copy.start()
            s_copy.start()
        g_copy.wait()

        @pl.loop(0, orb // 2)
        def _(pair):
            for slot in range(2):
                i = 2 * pair + slot
                block = gv[i].astype(jnp.float32).reshape(orb, pair_rows, LANES)
                spread(plain.at[slot], (block, block), repeat * ROWS)
                store_forms(plain.at[slot], gf, i, 4)

        s_copy.wait()

        @pl.loop(0, orb // 2)
        def _(pair):
            for slot in range(2):
                i = 2 * pair + slot
                blocks = [
                    sv[k, i].astype(jnp.float32).reshape(orb, pair_rows, LANES) for k in range(2)
                ]
                spread(plain.at[slot], blocks, pair_rows)
                store_forms(plain.at[slot], sf, i, 3)

    def keldysh_chunk(lc):
        if chunks > 1:
            prepare(lc)

        def products(ib, first_tile, last_tile):
            irows = pl.ds(ib * IBLOCK, IBLOCK)

            @pl.loop(0, (last_tile - first_tile) * jblocks, unroll=2)
            def _(step):
                tile, jb = first_tile + step // jblocks, lax.rem(step, jblocks)
                jrows = pl.ds(jb * JBLOCK, JBLOCK)
                source = green_tile(tile)
                total = [None] * 3
                for inner in range(orb):
                    for form in range(3):
                        term = gf[source, form, irows, inner][:, None] * sf[tile, form, inner, jrows][None]
                        total[form] = term if inner == 0 else total[form] + term
                real = total[0] - total[1]
                imag = total[2] - total[0] - total[1]
                for form, value in enumerate((real, imag, real + imag)):
                    hf[tile, form, :, jrows] = value

            @pl.loop(0, jblocks, unroll=2)
            def _(jb):
                jrows = pl.ds(jb * JBLOCK, JBLOCK)
                for tile in range(first_tile, last_tile):
                    source = tile if tile < repeat else tile - (repeat - edge_tiles)
                    total = [None] * 3
                    for inner in range(orb):
                        for form, other in enumerate((0, 1, 3)):
                            term = hf[tile, form, :, inner][:, None] * gf[source, other, jrows, inner][None]
                            total[form] = term if inner == 0 else total[form] + term
                    parts = (total[0] + total[1], total[2] - total[0] + total[1])
                    for c, value in enumerate(parts):
                        for t, row, size, k, energy in pieces(energies):
                            if t == tile:
                                start = halo + 2 * energy + c
                                ext[lc, k, irows, jrows, pl.ds(start, size, stride=2)] = value[
                                    :, :, row : row + size
                                ]

        @pl.loop(0, iblocks)
        def _(ib):
            irows = pl.ds(ib * IBLOCK, IBLOCK)
            products(ib, 0, edge_tiles)
            for side, start in enumerate((halo, pair_rows)):
                for k in range(2):
                    for j in range(orb):
                        row = (j % PACK) * halo
                        edge[side, k, :, j // PACK, row : row + halo] = ext[
                            lc, k, irows, j, start : start + halo
                        ]
                send[lc, side, ib] = edge[side].astype(jnp.bfloat16)
                halo_copy(lc, ib, side).start()

        if edge_tiles < tiles:
            @pl.loop(0, iblocks)
            def _(ib):
                products(ib, edge_tiles, tiles)

    if chunks == 1:
        prepare(0)
    pl.semaphore_wait(barrier, 2 + (nz - 1) + (ne - 1))

    @pl.loop(1, nz)
    def _(step):
        bond_copy(step).start()

    if chunks == 1:
        keldysh_chunk(0)
    else:
        pl.loop(0, chunks)(keldysh_chunk)

    def inner_traces(lc):
        def add_row(i, totals):
            result = []
            for offset, total in enumerate(totals, 1):
                size = pair_rows - 2 * offset
                ahead = ext[lc, 0, i, :, halo + 2 * offset : halo + pair_rows]
                behind = ext[lc, 1, :, i, halo : halo + size]
                result.append(total + jnp.sum(ahead * behind, axis=0))
            return tuple(result)

        starts = tuple(
            jnp.zeros((pair_rows - 2 * offset, LANES), jnp.float32)
            for offset in range(1, SHIFT + 1)
        )
        return lax.fori_loop(0, orb, add_row, starts, unroll=2)

    def signed_sum(total):
        parity = lax.rem(lax.broadcasted_iota(jnp.int32, total.shape, 0), 2)
        return jnp.sum(jnp.where(parity == 0, total, -total), axis=0, keepdims=True)

    def store_inner(lc):
        first[0, lc] = jnp.zeros((ROWS, LANES), jnp.float32)
        for offset, total in enumerate(inner_traces(lc)):
            if total.shape[0]:
                first[0, lc, offset : offset + 1] = signed_sum(total)

    if chunks == 1:
        store_inner(0)
    else:
        pl.loop(0, chunks)(store_inner)

    @pl.loop(1, nz)
    def _(step):
        bond_copy(step).wait()

    for lc in range(chunks):
        block = bonds[:, :, lc * LANES : (lc + 1) * LANES].reshape(atoms, LANES)
        mixing[lc] = block.astype(jnp.float32).T.astype(jnp.bfloat16)

    keep_high = (place != last).astype(jnp.float32)
    keep_low = (place != 0).astype(jnp.float32)

    def halo_rows(lc):
        def take_block(ib, totals):
            for side in range(2):
                halo_copy(lc, ib, side).wait()
            irows = pl.ds(ib * IBLOCK, IBLOCK)
            for side, keep in enumerate((keep_high, keep_low)):
                start = 0 if side else halo + pair_rows
                for k in range(2):
                    rows = recv[lc, side, ib, k].astype(jnp.float32) * keep
                    for j in range(orb):
                        row = (j % PACK) * halo
                        ext[lc, k, irows, j, start : start + halo] = rows[
                            :, j // PACK, row : row + halo
                        ]
            totals = list(totals)
            for step in range(IBLOCK):
                i = ib * IBLOCK + step
                for offset in range(1, SHIFT + 1):
                    ahead = ext[lc, 0, :, i, halo : halo + 2 * offset]
                    behind = ext[lc, 1, i, :, halo - 2 * offset : halo]
                    totals[offset - 1] += jnp.sum(ahead * behind, axis=0)
            return tuple(totals)

        starts = tuple(
            jnp.zeros((2 * offset, LANES), jnp.float32) for offset in range(1, SHIFT + 1)
        )
        totals = lax.fori_loop(0, iblocks, take_block, starts)
        for offset, total in enumerate(totals):
            first[0, lc, offset : offset + 1] += signed_sum(total)

    if chunks == 1:
        halo_rows(0)
    else:
        pl.loop(0, chunks)(halo_rows)

    def first_copy(step):
        return pltpu.make_async_remote_copy(
            src_ref=first.at[0],
            dst_ref=first.at[step],
            send_sem=fsend.at[step],
            recv_sem=frecv.at[step],
            device_id={"energy": e, "atom": lax.rem(z + step, nz)},
            device_id_type=MESH,
        )

    def second_copy(step):
        return pltpu.make_async_remote_copy(
            src_ref=second.at[0],
            dst_ref=second.at[step],
            send_sem=ssend.at[step],
            recv_sem=srecv.at[step],
            device_id={"energy": lax.rem(e + step, ne), "atom": z},
            device_id_type=MESH,
        )

    def shift_energies(k):
        upward, downward = (emission, absorption) if k == 0 else (absorption, emission)

        @pl.loop(0, orb, unroll=4)
        def _(i):
            mixed = None
            for lc in range(chunks):
                total = None
                for offset in range(1, SHIFT + 1):
                    for sign, factor in ((1, upward[offset - 1]), (-1, downward[offset - 1])):
                        start = halo + 2 * sign * offset
                        term = factor[None] * ext[lc, k, i, :, start : start + out_rows]
                        total = term if total is None else total + term
                flat = total.reshape(orb * out_rows, LANES).astype(jnp.bfloat16)
                product = jnp.dot(flat, mixing[lc], preferred_element_type=jnp.float32)
                mixed = product if mixed is None else mixed + product
            if out_rows != pair_rows:
                mixed = mixed.reshape(orb, out_rows, atoms)[:, :pair_rows]
                mixed = mixed.reshape(orb * pair_rows, atoms)
            result[k, i] = mixed.astype(jnp.bfloat16)

    def out_copy(k):
        return pltpu.make_async_copy(result.at[k], out.at[k], out_sem.at[k])

    @pl.loop(1, nz)
    def _(step):
        first_copy(step).start()

    shift_energies(0)
    out_copy(0).start()

    @pl.loop(1, nz)
    def _(step):
        first_copy(step).wait()

    second[0] = jnp.sum(first[...], axis=0)

    @pl.loop(1, ne)
    def _(step):
        second_copy(step).start()

    shift_energies(1)
    out_copy(1).start()

    @pl.loop(1, ne)
    def _(step):
        second_copy(step).wait()

    summed = jnp.sum(second[...], axis=0)
    own = jnp.zeros((ROWS, tile_width), jnp.float32)
    for tile in range(nz):
        lc, lane = divmod(tile * tile_width, LANES)
        own = jnp.where(z == tile, summed[lc, :, lane : lane + tile_width], own)
    share = modes // ne
    scale = 1.0 / math.sqrt(energies * ne * nz)
    for row in range(share):
        mode = e * share + row
        shift = shifts[0, mode]
        line = jnp.zeros((1, tile_width), jnp.float32)
        for level in range(1, SHIFT + 1):
            line += jnp.where(shift == level, 1.0, 0.0) * own[level - 1 : level]
        share_out[row : row + 1] = line * (coupling[0, mode] * scale)
    for k in range(2):
        out_copy(k).wait()


def copy_kernel(source, small_source, target, small_target, held, small_held, in_sems, out_sems):
    half = source.shape[1] // 2
    stages = [(small_source, small_held, small_target)]
    for k in range(2):
        for part in range(2):
            rows = pl.ds(part * half, half)
            stages.append((source.at[k, rows], held.at[k, rows], target.at[k, rows]))
    loads = [
        pltpu.make_async_copy(first, middle, in_sems.at[index])
        for index, (first, middle, last) in enumerate(stages)
    ]
    stores = [
        pltpu.make_async_copy(middle, last, out_sems.at[index])
        for index, (first, middle, last) in enumerate(stages)
    ]
    for load in loads:
        load.start()
    for load, store in zip(loads, stores):
        load.wait()
        store.start()
    for store in stores:
        store.wait()


def local(ne, nz, green_ret, broadening, coupling, occupation, shifts, neighbours, bond_count, bond_weight):
    orb, energies, atoms = green_ret.shape[1], green_ret.shape[3], green_ret.shape[4]
    modes, slots = coupling.shape[0], neighbours.shape[1]
    tile_width = neighbours.shape[0]
    chunks = atoms // LANES
    pair_rows = 2 * energies
    tiles = pl.cdiv(pair_rows, ROWS)
    out_rows = ceil_to(pair_rows, ROWS)
    ext_rows = ceil_to(max(pair_rows, out_rows) + 4 * SHIFT, ROWS)
    iblocks = orb // IBLOCK
    edge_shape = (2, IBLOCK, orb // PACK, PACK * 2 * SHIFT, LANES)
    halo_shape = (chunks, 2, iblocks) + edge_shape
    dma = pltpu.SemaphoreType.DMA
    vmem = pl.BlockSpec(memory_space=pltpu.VMEM)
    hbm = pl.BlockSpec(memory_space=pltpu.HBM)
    green = green_ret.transpose(1, 2, 3, 0, 4).reshape(orb, orb * pair_rows, atoms)
    broad = broadening.transpose(0, 2, 3, 4, 1, 5).reshape(2, orb, orb * pair_rows, atoms)
    out, pol = pl.pallas_call(
        functools.partial(keldysh_kernel, ne, nz, orb, energies, atoms, modes, slots),
        out_shape=(
            jax.ShapeDtypeStruct((2, orb, orb * pair_rows, atoms), jnp.bfloat16),
            jax.ShapeDtypeStruct((modes // ne, tile_width), jnp.float32),
        ),
        in_specs=[hbm] * 8,
        out_specs=(hbm, vmem),
        scratch_shapes=[
            pltpu.VMEM((orb, orb * pair_rows, LANES), jnp.bfloat16),
            pltpu.VMEM((2, orb, orb * pair_rows, LANES), jnp.bfloat16),
            pltpu.VMEM((2, orb, 2 * pair_rows, LANES), jnp.float32),
            pltpu.VMEM((green_tiles(energies), 4, orb, orb, ROWS, LANES), jnp.float32),
            pltpu.VMEM((tiles, 3, orb, orb, ROWS, LANES), jnp.float32),
            pltpu.VMEM((tiles, 3, IBLOCK, orb, ROWS, LANES), jnp.float32),
            pltpu.VMEM((chunks, 2, orb, orb, ext_rows, LANES), jnp.float32),
            pltpu.VMEM((2,) + edge_shape, jnp.float32),
            pltpu.VMEM(halo_shape, jnp.bfloat16),
            pltpu.VMEM(halo_shape, jnp.bfloat16),
            pltpu.VMEM((nz, tile_width, atoms), jnp.bfloat16),
            pltpu.VMEM((chunks, LANES, atoms), jnp.bfloat16),
            pltpu.VMEM((2, orb, orb * pair_rows, atoms), jnp.bfloat16),
            pltpu.VMEM((nz, chunks, ROWS, LANES), jnp.float32),
            pltpu.VMEM((ne, chunks, ROWS, LANES), jnp.float32),
            pltpu.VMEM((2, 1, modes), jnp.float32),
            pltpu.VMEM((1, modes), jnp.int32),
            pltpu.SMEM((1, modes), jnp.float32),
            pltpu.SMEM((1, modes), jnp.int32),
            pltpu.SMEM((tile_width,), jnp.int32),
            pltpu.VMEM(neighbours.shape, jnp.int32),
            pltpu.VMEM(bond_weight.shape, jnp.bfloat16),
            dma((8,)),
            dma((2,)),
            dma,
            dma,
            dma((chunks, 2, iblocks)),
            dma((chunks, 2, iblocks)),
            dma((nz,)),
            dma((nz,)),
            dma((nz,)),
            dma((nz,)),
            dma((ne,)),
            dma((ne,)),
        ],
        compiler_params=pltpu.CompilerParams(
            collective_id=0, has_side_effects=True, vmem_limit_bytes=64 * 1024 * 1024
        ),
    )(
        green,
        broad,
        coupling.reshape(1, modes),
        occupation.reshape(1, modes),
        shifts.reshape(1, modes),
        bond_count,
        neighbours,
        bond_weight,
    )
    out, pol = pl.pallas_call(
        copy_kernel,
        out_shape=(
            jax.ShapeDtypeStruct(out.shape, out.dtype),
            jax.ShapeDtypeStruct(pol.shape, pol.dtype),
        ),
        in_specs=[hbm] * 2,
        out_specs=(hbm, hbm),
        scratch_shapes=[
            pltpu.VMEM(out.shape, out.dtype),
            pltpu.VMEM(pol.shape, pol.dtype),
            dma((5,)),
            dma((5,)),
        ],
        compiler_params=pltpu.CompilerParams(vmem_limit_bytes=64 * 1024 * 1024),
    )(out, pol)
    self_energy = out.reshape(2, orb, orb, energies, 2, atoms).transpose(0, 4, 1, 2, 3, 5)
    return self_energy, pol


def solution(mesh):
    in_specs = (
        P(None, None, None, ("energy", "atom"), None),
        P(None, None, None, None, ("energy", "atom"), None),
        P(),
        P(),
        P(),
        P("atom", None),
        P("atom"),
        P("atom", None),
    )
    out_specs = (P(None, None, None, None, ("energy", "atom"), None), P("energy", "atom"))
    body = functools.partial(local, mesh.shape["energy"], mesh.shape["atom"])
    return jax.shard_map(body, mesh=mesh, in_specs=in_specs, out_specs=out_specs, check_vma=False)
```
